128 devices in a mesh: au: 16 (over x, y), vert: 8 (over z, core).
Axes of the slice: x: 4, y: 4, z: 4, core: 2. Of those that a mesh axis runs over, the one named last changes fastest.
Arguments:
- visibility: bfloat16 [262144, 128], P(('au', 'vert')), may hold values from -6 to 6
- destination: int32 [262144, 1], P(('au', 'vert')), may hold values from 0 to 127; in each aligned block of 2048 rows (0 to 2047, 2048 to 4095, ...) at most 32 rows name the same one
- cell_u: int32 [262144], P(('au', 'vert')), may hold values from 0 to 127
- cell_v: int32 [262144], P(('au', 'vert')), may hold values from 0 to 127
- tap_u: int32 [262144], P(('au', 'vert')), may hold values from 0 to 127
- tap_v: int32 [262144], P(('au', 'vert')), may hold values from 0 to 127
- kernel_table: bfloat16 [128, 8], replicated, may hold values from 0.19921875 to 1
Outputs:
- uv_grid: float32 [2048, 1024, 128], P('au', 'vert')
The draws below stay inside these ranges and needn't reach their ends.
Inputs may be any that keep to these rules, and one draw needn't show every extreme that they name: `destination`: of the 2048 rows of one device, at most 32 name the same tile, and in every draw some device sends exactly 32 rows to some tile.
All inputs are finite; a program needn't handle non-finite values.
Results may differ from the reference program's by a relative error of at most 0.0029.
Values may be sent and summed in bfloat16 or wider, within the bound.
No kernel may reach another device: no remote copies, remote signals or barrier semaphores. Data moves between devices by JAX's collectives and lax.ppermute only.
A program may use at most 128 MiB of HBM per device.

```python
import math
import jax
import jax.numpy as jnp
import numpy as np
from jax import lax

FEAT = 128
TAPS = 8
OVER = 128
TU = 128
TV = 128
RB = 2048
CAP = 32
ROWS = 262144
NU = 2048
NV = 1024
N_VERT = 8
DEVICES = 128


def touch_ends(entries, rng, least, largest):
    extent = entries.shape
    place = [jax.random.randint(jax.random.fold_in(rng, axis), (), 0, extent[axis]) for axis in range(len(extent))]
    entries = entries.at[tuple(place)].set(least)
    longest = extent.index(max(extent))
    place[longest] = (place[longest] + 1) % extent[longest]
    return entries.at[tuple(place)].set(largest)


def level_of(stream_key, dims, shards, low, high):
    def one(axis_at, shards_of):
        heights = jax.random.uniform(jax.random.fold_in(jax.random.fold_in(stream_key, 6), axis_at), (shards_of,), jnp.float32, low / len(shards), high / len(shards))
        return jnp.repeat(jnp.exp(heights), dims[axis_at] // shards_of).reshape((-1,) + (1,) * (len(dims) - axis_at - 1))

    loudness = one(*shards[0])
    for cut in shards[1:]:
        loudness = loudness * one(*cut)
    return loudness


def deal_out(stream_key, own, number, rows, count, top, bound, skew):
    sequence = jax.random.permutation(stream_key, count)
    crowded, ordinary = shares(count, rows * top, bound, skew, True), shares(count, rows * top, bound, skew, False)
    places = jnp.arange(count)

    def named(lengths, offset_by):
        used = int((lengths > 0).sum())
        fixed = max(1, used // 4)
        passed = fixed + (places - fixed + offset_by * (used - fixed)) % max(1, count - fixed)
        return jnp.zeros((count,), jnp.int32).at[sequence[jnp.where(places < fixed, places, passed)]].set(jnp.asarray(lengths, jnp.int32))

    lengths = jnp.where(number % 4 == 0, named(crowded, number // 4), named(ordinary, number - number // 4 - 1))
    mixed = jax.random.permutation(jax.random.fold_in(own, 3), count)
    giver, taker = mixed[0:count // 2 * 2:2], mixed[1:count // 2 * 2:2]
    margin = jnp.minimum(lengths[giver] - 1, bound - lengths[taker]) // 2
    margin = jnp.where((giver == sequence[0]) | (taker == sequence[0]) | (lengths[taker] == 0), 0, jnp.maximum(margin, 0))
    passed = jax.random.randint(jax.random.fold_in(own, 4), (count // 2,), 0, 1 << 20) % (margin + 1)
    lengths = lengths.at[giver].add(-passed).at[taker].add(passed)
    items = jnp.searchsorted(jnp.cumsum(lengths), jnp.arange(rows * top), side="right").astype(jnp.int32)
    table = items.reshape(top, rows).T
    table = table[jax.random.permutation(jax.random.fold_in(own, 1), rows)]
    offset_by = jax.random.randint(jax.random.fold_in(own, 2), (rows, 1), 0, top)
    return jnp.take_along_axis(table, (jnp.arange(top)[None, :] + offset_by) % top, axis=1)


def shares(number_of, total, bound, slope, full):
    portions = [(1 << 20) // math.isqrt(rank ** slope) + 1 for rank in range(1, number_of + 1)]
    largest = bound if full else min(bound, max(-(-total // number_of), total * portions[0] // sum(portions)))
    least = 1 if total - largest >= number_of - 1 else 0
    counts, surplus = [largest] + [least] * (number_of - 1), total - largest - least * (number_of - 1)
    while surplus > 0:
        movable = [i for i in range(1, number_of) if counts[i] < largest] or [i for i in range(1, number_of) if counts[i] < bound]
        pool, left = sum([portions[i] for i in movable]), surplus
        for i in movable:
            more = min(bound - counts[i], max(1, left * portions[i] // pool), surplus)
            counts[i] = counts[i] + more
            surplus = surplus - more
    return np.array(counts)


def scatter_about(stream_key, dims, deviation, reach, split=(), kind=jnp.bfloat16):
    array = jax.random.normal(stream_key, dims, jnp.float32) * deviation
    if len(split) > 0:
        array = level_of(stream_key, dims, split, -0.22, 0.18) * array
    return jnp.clip(array, min=-reach, max=reach).astype(kind)


def setup_inputs(seed: int = 0) -> dict:
    keys = jax.random.split(jax.random.key(seed), 8)
    visibility = scatter_about(keys[0], (ROWS, FEAT), 1.0, 6.0, ((0, 128),))
    destination_keys = jax.random.split(jax.random.fold_in(keys[1], 1), ROWS // RB)
    destination_turns = jax.random.permutation(jax.random.fold_in(keys[1], 3), ROWS // RB)
    destination = jax.vmap(lambda own, number: deal_out(jax.random.fold_in(keys[1], 2), own, number, RB, DEVICES, 1, CAP, 2))(destination_keys, destination_turns).reshape((ROWS, 1))
    cell_u = touch_ends(jax.random.randint(keys[2], (ROWS,), 0, TU), jax.random.fold_in(keys[2], 1), 0, TU - 1).astype(jnp.int32)
    cell_v = touch_ends(jax.random.randint(keys[3], (ROWS,), 0, TV), jax.random.fold_in(keys[3], 1), 0, TV - 1).astype(jnp.int32)
    tap_u = touch_ends(jax.random.randint(keys[4], (ROWS,), 0, OVER), jax.random.fold_in(keys[4], 1), 0, OVER - 1).astype(jnp.int32)
    tap_v = touch_ends(jax.random.randint(keys[5], (ROWS,), 0, OVER), jax.random.fold_in(keys[5], 1), 0, OVER - 1).astype(jnp.int32)
    kernel_table = jnp.clip(jax.random.uniform(keys[6], (OVER, TAPS), jnp.float32, 0.19921875, 1.0), 0.19921875, 1.0).astype(jnp.bfloat16)
    return {"visibility": visibility, "destination": destination, "cell_u": cell_u, "cell_v": cell_v, "tap_u": tap_u, "tap_v": tap_v, "kernel_table": kernel_table}


def reference(visibility, destination, cell_u, cell_v, tap_u, tap_v, kernel_table):
    dest = destination[:, 0]
    tile_u = dest // N_VERT
    tile_v = dest % N_VERT
    base_u = (tile_u * TU + cell_u).astype(jnp.int32)
    base_v = (tile_v * TV + cell_v).astype(jnp.int32)
    blocks = ROWS // RB
    table = kernel_table.astype(jnp.float32)
    steps_in = (visibility.reshape(blocks, RB, FEAT), base_u.reshape(blocks, RB), base_v.reshape(blocks, RB),
                tap_u.reshape(blocks, RB), tap_v.reshape(blocks, RB))
    taps_range = jnp.arange(TAPS, dtype=jnp.int32)

    def one_block(grid, items):
        vis, start_u, start_v, phase_u, phase_v = items
        ku = table[phase_u]
        kv = table[phase_v]
        weighted = (kv[:, :, None] * vis.astype(jnp.float32)[:, None, :]).astype(jnp.bfloat16)
        weighted = lax.optimization_barrier(weighted).astype(jnp.float32)
        contrib = ku[:, :, None, None] * weighted[:, None, :, :]
        index_u = start_u[:, None] + taps_range[None, :]
        index_v = start_v[:, None] + taps_range[None, :]
        grid = grid.at[index_u[:, :, None], index_v[:, None, :]].add(contrib)
        return grid, None

    grid = jnp.zeros((NU + 8, NV + 8, FEAT), jnp.float32)
    grid, unused = lax.scan(one_block, grid, steps_in)
    return grid[4:NU + 4, 4:NV + 4]
```

```python
import jax
import jax.numpy as jnp
from jax import lax
from jax.experimental import pallas as pl
from jax.experimental.pallas import tpu as pltpu
from jax.sharding import PartitionSpec as P

FEAT = 128
TAPS = 8
TU = 128
TV = 128
CAP = 32
SENT = CAP + 8
BLK = 256
EU = 144
EV = 144
PAD = 4
GROUP = 4
VMEM_LIMIT = 56 * 1024 * 1024
NT = (((1,), (1,)), ((), ()))

f32 = jnp.float32
bf16 = jnp.bfloat16
i32 = jnp.int32


def iota(shape, dim):
    return lax.broadcasted_iota(i32, shape, dim)


def dot(a, b):
    return jnp.dot(a, b, preferred_element_type=f32)


def earlier(n):
    return (iota((n, n), 0) < iota((n, n), 1)).astype(f32).astype(bf16)


def pack_kernel(dest_ref, cu_ref, cv_ref, tu_ref, tv_ref, vis_ref, out_ref, slot_v, slot_s, xf, packed, meta, sem):
    rows = vis_ref.shape[0]
    tiles = out_ref.shape[0]
    blocks = rows // BLK
    before = earlier(BLK)
    base = jnp.zeros((tiles, 1), f32)
    placed = jnp.zeros((tiles, 4 * CAP), f32)
    tile_ids = iota((tiles, BLK), 0)
    cap_ids = iota((CAP, BLK), 0)
    for b in range(blocks):
        part = pl.ds(b * BLK, BLK)
        d = dest_ref[:, part]
        mine = (tile_ids == d).astype(f32)
        mine16 = mine.astype(bf16)
        rank = jnp.sum(mine * (dot(mine16, before) + base), 0, keepdims=True).astype(i32)
        base = base + jnp.sum(mine, 1, keepdims=True)
        slot_v[pl.ds(b, 1), :] = d * CAP + rank
        at = cap_ids == rank
        fields = [
            jnp.where(at, (ref[:, part] + 1).astype(f32), 0.0)
            for ref in (cu_ref, cv_ref, tu_ref, tv_ref)
        ]
        fields = jnp.concatenate(fields, 0).astype(bf16)
        placed = placed + lax.dot_general(mine16, fields, NT, preferred_element_type=f32)
    meta[...] = placed
    copy = pltpu.make_async_copy(slot_v, slot_s, sem)
    copy.start()

    @pl.loop(0, tiles)
    def _(t):
        packed[pl.ds(t * CAP, CAP), :] = jnp.zeros((CAP, FEAT), f32)

    @pl.loop(0, rows // 32)
    def _(t):
        part = pl.ds(t * 32, 32)
        xf[part, :] = vis_ref[part, :].astype(f32)

    copy.wait()
    step = 32

    for b in range(blocks):

        @pl.loop(0, BLK // step)
        def _(t):
            for j in range(step):
                at = t * step + j
                packed[pl.ds(slot_s[b, at], 1), :] = xf[pl.ds(b * BLK + at, 1), :]

    @pl.loop(0, tiles)
    def _(t):
        rows_t = packed[pl.ds(t * CAP, CAP), :]
        meta_t = jnp.broadcast_to(meta[pl.ds(t, 1), :], (SENT - CAP, FEAT))
        out_ref[t] = jnp.concatenate([rows_t, meta_t], 0).astype(bf16)


def pack(visibility, destination, cell_u, cell_v, tap_u, tap_v, tiles):
    rows = visibility.shape[0]
    row = lambda x: x.reshape(1, rows)
    return pl.pallas_call(
        pack_kernel,
        out_shape=jax.ShapeDtypeStruct((tiles, SENT, FEAT), bf16),
        scratch_shapes=[
            pltpu.VMEM((rows // BLK, BLK), i32),
            pltpu.SMEM((rows // BLK, BLK), i32),
            pltpu.VMEM((rows, FEAT), f32),
            pltpu.VMEM((tiles * CAP, FEAT), f32),
            pltpu.VMEM((tiles, FEAT), f32),
            pltpu.SemaphoreType.DMA(()),
        ],
        compiler_params=pltpu.CompilerParams(vmem_limit_bytes=VMEM_LIMIT),
        name="pack_rows",
    )(row(destination), row(cell_u), row(cell_v), row(tap_u), row(tap_v), visibility)


def grid_kernel(
    recv_ref, table_ref, out_hbm, ve_ref, ue_ref,
    xf, xm, xs, ms, meta, meta_t, pos_v, pos_s, span_v, span_s, grid, stage, sems, out_sems,
):
    sources = recv_ref.shape[0]
    slots = sources * CAP
    blocks = slots // BLK
    lanes = BLK // sources

    @pl.loop(0, sources)
    def _(s):
        x = recv_ref[s].astype(f32)
        xf[pl.ds(s * CAP, CAP), :] = x[:CAP]
        meta[pl.ds(s, 1), :] = x[CAP:CAP + 1]

    placed = meta[...]
    meta_t[...] = placed.T
    keys = 64

    def key_row(b):
        out = []
        for k in range(b * lanes, (b + 1) * lanes):
            cu1 = meta_t[pl.ds(k, 1), :].astype(i32)
            cv1 = meta_t[pl.ds(CAP + k, 1), :].astype(i32)
            out.append(jnp.where(cu1 > 0, (cv1 - 1) >> 1, keys))
        return jnp.concatenate(out, 1)

    key_ids = iota((128, BLK), 0)
    total = jnp.zeros((128, BLK), f32)
    for b in range(blocks):
        total = total + (key_ids == key_row(b)).astype(f32)
    total = jnp.broadcast_to(jnp.sum(total, 1, keepdims=True), (128, 128))
    below = (iota((128, 128), 1) < iota((128, 128), 0)).astype(f32).astype(bf16)
    high = jnp.floor(total * (1.0 / 64.0))
    low = total - 64.0 * high
    start = 64.0 * dot(below, high.astype(bf16)) + dot(below, low.astype(bf16))
    count = start[keys:keys + 1, :]
    lane = iota((128, 128), 1).astype(f32) * BLK
    real = iota((128, 128), 0) < keys
    first = jnp.sum(jnp.where(real & (start + total <= lane), 1.0, 0.0), 0, keepdims=True)
    last = jnp.sum(jnp.where(real & (start < jnp.minimum(lane + BLK, count)), 1.0, 0.0), 0, keepdims=True) - 1.0
    span_v[...] = jnp.concatenate([first, last, count, jnp.zeros((5, 128), f32)], 0).astype(i32)
    span_copy = pltpu.make_async_copy(span_v, span_s, sems.at[0])
    span_copy.start()
    before = earlier(BLK)
    base = start[:, 0:1]
    for b in range(blocks):
        mine = (key_ids == key_row(b)).astype(f32)
        pos = jnp.sum(mine * (dot(mine.astype(bf16), before) + base), 0, keepdims=True)
        pos_v[pl.ds(b, 1), :] = pos.astype(i32)
        base = base + jnp.sum(mine, 1, keepdims=True)
    pos_copy = pltpu.make_async_copy(pos_v, pos_s, sems.at[1])
    pos_copy.start()
    for k in range(CAP):
        xm[pl.ds(k * sources, sources), :] = pltpu.roll(placed, (FEAT - k) % FEAT, 1)

    @pl.loop(0, EV)
    def _(t):
        grid[pl.ds(t * EU, EU), :] = jnp.zeros((EU, FEAT), f32)

    pos_copy.wait()
    span_copy.wait()

    @pl.loop(0, sources)
    def _(s):
        for k in range(CAP):
            p = pos_s[k // lanes, (k % lanes) * sources + s]
            xs[pl.ds(p, 1), :] = xf[pl.ds(s * CAP + k, 1), :]
            ms[pl.ds(p, 1), :] = xm[pl.ds(k * sources + s, 1), :]

    table_tr = table_ref[...]
    pick = (iota((8, FEAT), 1) == CAP * iota((8, FEAT), 0)).astype(f32).astype(bf16)
    phase_ids = iota((128, BLK), 0)
    u_ids = iota((EU, BLK), 0)
    t_ids = iota((8, BLK), 0)

    @pl.loop(0, (span_s[2, 0] + BLK - 1) // BLK)
    def _(c):
        part = pl.ds(c * BLK, BLK)
        fields = lax.dot_general(pick, ms[part, :].astype(bf16), NT, preferred_element_type=f32).astype(i32) - 1
        cu, cv, tu, tv = (fields[i:i + 1] for i in range(4))
        ku = dot(table_tr, (phase_ids == tu).astype(f32).astype(bf16))
        kv = dot(table_tr, (phase_ids == tv).astype(f32).astype(bf16))
        off = u_ids - (cu + 4)
        wu = jnp.zeros((EU, BLK), f32)
        for a in range(TAPS):
            wu = jnp.where(off == a, ku[a:a + 1], wu)
        wu = wu.astype(bf16)
        v_first = 2 * span_s[0, c]
        steps = 2 * (span_s[1, c] - span_s[0, c]) + TAPS + 1

        @pl.loop(0, (steps + GROUP - 1) // GROUP)
        def _(g):
            v_at = v_first + g * GROUP
            off_v = (t_ids + v_at) - cv
            wv = jnp.zeros((8, BLK), f32)
            for a in range(TAPS):
                wv = jnp.where(off_v == a, kv[a:a + 1], wv)
            wv = wv.T
            x = xs[part, :]
            for j in range(0, GROUP, 2):
                rhs = jnp.concatenate([x * wv[:, j:j + 1], x * wv[:, j + 1:j + 2]], 1).astype(bf16)
                add = dot(wu, rhs)
                for i in range(2):
                    at = pl.ds((v_at + j + i) * EU, EU)
                    grid[at, :] = grid[at, :] + add[:, i * FEAT:(i + 1) * FEAT]

    ve_ref[0] = grid[pl.ds(0, PAD * EU), :]
    ve_ref[1] = grid[pl.ds((TV + PAD) * EU, PAD * EU), :]

    def turned(u):
        return [grid[pl.ds((PAD + 8 * t) * EU + u, 8, stride=EU), :] for t in range(TV // 8)]

    for u in range(PAD):
        for e, at in enumerate((PAD + u, TU + 8 + u)):
            ue_ref[e, u] = jnp.concatenate(turned(at), 0)

    many = 8

    def out_copy(t, slot):
        return pltpu.make_async_copy(stage.at[slot], out_hbm.at[pl.ds(t * many, many)], out_sems.at[slot])

    @pl.loop(0, TU // many)
    def _(t):
        slot = t % 2

        @pl.when(t >= 2)
        def _():
            out_copy(t - 2, slot).wait()

        for u in range(many):
            stage[slot, u] = jnp.concatenate(turned(8 + t * many + u), 0)
        out_copy(t, slot).start()

    for t in (TU // many - 2, TU // many - 1):
        out_copy(t, t % 2).wait()


def grid_rows(recv, table):
    sources = recv.shape[0]
    slots = sources * CAP
    vmem = pl.BlockSpec(memory_space=pltpu.VMEM)
    return pl.pallas_call(
        grid_kernel,
        in_specs=[vmem, vmem],
        out_specs=(pl.BlockSpec(memory_space=pl.ANY), vmem, vmem),
        out_shape=(
            jax.ShapeDtypeStruct((TU, TV, FEAT), f32),
            jax.ShapeDtypeStruct((2, PAD * EU, FEAT), f32),
            jax.ShapeDtypeStruct((2, PAD, TV, FEAT), f32),
        ),
        scratch_shapes=[
            pltpu.VMEM((slots, FEAT), f32),
            pltpu.VMEM((slots, FEAT), f32),
            pltpu.VMEM((slots, FEAT), f32),
            pltpu.VMEM((slots, FEAT), f32),
            pltpu.VMEM((sources, FEAT), f32),
            pltpu.VMEM((FEAT, sources), f32),
            pltpu.VMEM((slots // BLK, BLK), i32),
            pltpu.SMEM((slots // BLK, BLK), i32),
            pltpu.VMEM((8, 128), i32),
            pltpu.SMEM((8, 128), i32),
            pltpu.VMEM((EV * EU, FEAT), f32),
            pltpu.VMEM((2, 8, TV, FEAT), f32),
            pltpu.SemaphoreType.DMA((2,)),
            pltpu.SemaphoreType.DMA((2,)),
        ],
        compiler_params=pltpu.CompilerParams(vmem_limit_bytes=VMEM_LIMIT),
        name="grid_rows",
    )(recv, table)


def shifted(x, axis, up):
    n = lax.axis_size(axis)
    pairs = [(i, i + 1) if up else (i + 1, i) for i in range(n - 1)]
    return lax.ppermute(x, axis, pairs)


def local(visibility, destination, cell_u, cell_v, tap_u, tap_v, kernel_table):
    axes = ("au", "vert")
    tiles = lax.axis_size("au") * lax.axis_size("vert")
    sent = pack(visibility, destination, cell_u, cell_v, tap_u, tap_v, tiles)
    recv = lax.all_to_all(sent, axes, split_axis=0, concat_axis=0, tiled=True)
    out, ve, ue = grid_rows(recv, kernel_table.T)
    v_low = shifted(ve[1], "vert", True).reshape(PAD, EU, FEAT).transpose(1, 0, 2)
    v_high = shifted(ve[0], "vert", False).reshape(PAD, EU, FEAT).transpose(1, 0, 2)
    for e, at in enumerate((PAD, TU + 8)):
        ue = ue.at[e, :, 0:PAD].add(v_low[at:at + PAD])
        ue = ue.at[e, :, TV - PAD:TV].add(v_high[at:at + PAD])
    u_low = shifted(ue[1], "au", True)
    u_high = shifted(ue[0], "au", False)
    out = out.at[:, 0:PAD].add(v_low[8:8 + TU])
    out = out.at[:, TV - PAD:TV].add(v_high[8:8 + TU])
    out = out.at[0:PAD].add(u_low)
    out = out.at[TU - PAD:TU].add(u_high)
    return out


def solution(mesh):
    rows = P(("au", "vert"))
    return jax.shard_map(
        local,
        mesh=mesh,
        in_specs=(P(("au", "vert"), None), P(("au", "vert"), None), rows, rows, rows, rows, P()),
        out_specs=P("au", "vert", None),
        check_vma=False,
    )
```

```python
import jax
import jax.numpy as jnp
from jax import lax
from jax.experimental import pallas as pl
from jax.experimental.pallas import tpu as pltpu
from jax.sharding import PartitionSpec as P

FEAT = 128
TAPS = 8
TU = 128
TV = 128
CAP = 32
SENT = CAP + 8
BLK = 256
EU = 144
EV = 160
PAD = 4
GROUP = 20
MIB = 1024 * 1024
NT = (((1,), (1,)), ((), ()))

f32 = jnp.float32
bf16 = jnp.bfloat16
i32 = jnp.int32


def iota(shape, dim):
    return lax.broadcasted_iota(i32, shape, dim)


def dot(a, b):
    return jnp.dot(a, b, preferred_element_type=f32)


def earlier(n):
    return (iota((n, n), 0) < iota((n, n), 1)).astype(f32).astype(bf16)


def pack_kernel(dest_ref, cu_ref, cv_ref, tu_ref, tv_ref, vis_ref, out_ref, slot_v, slot_s, xf, packed, meta, sem):
    rows = vis_ref.shape[0]
    tiles = out_ref.shape[0]
    blocks = rows // BLK
    before = earlier(BLK)
    base = jnp.zeros((tiles, 1), f32)
    placed = jnp.zeros((tiles, 4 * CAP), f32)
    tile_ids = iota((tiles, BLK), 0)
    cap_ids = iota((CAP, BLK), 0)
    for b in range(blocks):
        part = pl.ds(b * BLK, BLK)
        d = dest_ref[:, part]
        mine = (tile_ids == d).astype(f32)
        mine16 = mine.astype(bf16)
        rank = jnp.sum(mine * (dot(mine16, before) + base), 0, keepdims=True).astype(i32)
        base = base + jnp.sum(mine, 1, keepdims=True)
        slot_v[pl.ds(b, 1), :] = d * CAP + rank
        at = cap_ids == rank
        fields = [
            jnp.where(at, (ref[:, part] + 1).astype(f32), 0.0)
            for ref in (cu_ref, cv_ref, tu_ref, tv_ref)
        ]
        fields = jnp.concatenate(fields, 0).astype(bf16)
        placed = placed + lax.dot_general(mine16, fields, NT, preferred_element_type=f32)
    meta[...] = placed
    copy = pltpu.make_async_copy(slot_v, slot_s, sem)
    copy.start()

    @pl.loop(0, tiles)
    def _(t):
        packed[pl.ds(t * CAP, CAP), :] = jnp.zeros((CAP, FEAT), f32)

    @pl.loop(0, rows // 32)
    def _(t):
        part = pl.ds(t * 32, 32)
        xf[part, :] = vis_ref[part, :].astype(f32)

    copy.wait()
    step = 32

    for b in range(blocks):

        @pl.loop(0, BLK // step)
        def _(t):
            for j in range(step):
                at = t * step + j
                packed[pl.ds(slot_s[b, at], 1), :] = xf[pl.ds(b * BLK + at, 1), :]

    @pl.loop(0, tiles)
    def _(t):
        rows_t = packed[pl.ds(t * CAP, CAP), :]
        meta_t = jnp.broadcast_to(meta[pl.ds(t, 1), :], (SENT - CAP, FEAT))
        out_ref[t] = jnp.concatenate([rows_t, meta_t], 0).astype(bf16)


def pack(visibility, destination, cell_u, cell_v, tap_u, tap_v, tiles):
    rows = visibility.shape[0]
    row = lambda x: x.reshape(1, rows)
    return pl.pallas_call(
        pack_kernel,
        out_shape=jax.ShapeDtypeStruct((tiles, SENT, FEAT), bf16),
        scratch_shapes=[
            pltpu.VMEM((rows // BLK, BLK), i32),
            pltpu.SMEM((rows // BLK, BLK), i32),
            pltpu.VMEM((rows, FEAT), f32),
            pltpu.VMEM((tiles * CAP, FEAT), f32),
            pltpu.VMEM((tiles, FEAT), f32),
            pltpu.SemaphoreType.DMA(()),
        ],
        compiler_params=pltpu.CompilerParams(vmem_limit_bytes=16 * MIB),
        name="pack_rows",
    )(row(destination), row(cell_u), row(cell_v), row(tap_u), row(tap_v), visibility)


def grid_kernel(
    recv_ref, table_ref, out_hbm, ve_low, ve_high, ue_ref,
    xf, xm, xs, ms, meta, meta_t, pos_v, pos_s, span_v, span_s, wu, taps_v, grid3, sems, out_sems,
):
    grid = grid3.reshape(EV * EU, FEAT)
    sources = recv_ref.shape[0]
    slots = sources * CAP
    blocks = slots // BLK
    lanes = BLK // sources

    @pl.loop(0, sources)
    def _(s):
        x = recv_ref[s].astype(f32)
        xf[pl.ds(s * CAP, CAP), :] = x[:CAP]
        meta[pl.ds(s, 1), :] = x[CAP:CAP + 1]

    placed = meta[...]
    meta_t[...] = placed.T
    keys = 64

    def key_row(b):
        out = []
        for k in range(b * lanes, (b + 1) * lanes):
            cu1 = meta_t[pl.ds(k, 1), :].astype(i32)
            cv1 = meta_t[pl.ds(CAP + k, 1), :].astype(i32)
            out.append(jnp.where(cu1 > 0, (cv1 - 1) >> 1, keys))
        return jnp.concatenate(out, 1)

    key_ids = iota((128, BLK), 0)
    total = jnp.zeros((128, BLK), f32)
    for b in range(blocks):
        total = total + (key_ids == key_row(b)).astype(f32)
    total = jnp.broadcast_to(jnp.sum(total, 1, keepdims=True), (128, 128))
    below = (iota((128, 128), 1) < iota((128, 128), 0)).astype(f32).astype(bf16)
    high = jnp.floor(total * (1.0 / 64.0))
    low = total - 64.0 * high
    start = 64.0 * dot(below, high.astype(bf16)) + dot(below, low.astype(bf16))
    count = start[keys:keys + 1, :]
    lane = iota((128, 128), 1).astype(f32) * BLK
    real = iota((128, 128), 0) < keys
    first = jnp.sum(jnp.where(real & (start + total <= lane), 1.0, 0.0), 0, keepdims=True)
    last = jnp.sum(jnp.where(real & (start < jnp.minimum(lane + BLK, count)), 1.0, 0.0), 0, keepdims=True) - 1.0
    span_v[...] = jnp.concatenate([first, last, count, jnp.zeros((5, 128), f32)], 0).astype(i32)
    span_copy = pltpu.make_async_copy(span_v, span_s, sems.at[0])
    span_copy.start()
    before = earlier(BLK)
    base = start[:, 0:1]
    for b in range(blocks):
        mine = (key_ids == key_row(b)).astype(f32)
        pos = jnp.sum(mine * (dot(mine.astype(bf16), before) + base), 0, keepdims=True)
        pos_v[pl.ds(b, 1), :] = pos.astype(i32)
        base = base + jnp.sum(mine, 1, keepdims=True)
    pos_copy = pltpu.make_async_copy(pos_v, pos_s, sems.at[1])
    pos_copy.start()
    for k in range(CAP):
        xm[pl.ds(k * sources, sources), :] = pltpu.roll(placed, (FEAT - k) % FEAT, 1)

    @pl.loop(0, EV)
    def _(t):
        grid[pl.ds(t * EU, EU), :] = jnp.zeros((EU, FEAT), f32)

    pos_copy.wait()
    span_copy.wait()

    @pl.loop(0, sources)
    def _(s):
        for k in range(CAP):
            p = pos_s[k // lanes, (k % lanes) * sources + s]
            xs[pl.ds(p, 1), :] = xf[pl.ds(s * CAP + k, 1), :]
            ms[pl.ds(p, 1), :] = xm[pl.ds(k * sources + s, 1), :]

    table_tr = table_ref[...]
    pick = (iota((8, FEAT), 1) == CAP * iota((8, FEAT), 0)).astype(f32).astype(bf16)
    phase_ids = iota((128, BLK), 0)
    u_ids = iota((EU, BLK), 0)
    t_ids = iota((GROUP + 4, BLK), 0)
    chunks = (span_s[2, 0] + BLK - 1) // BLK

    @pl.loop(0, chunks)
    def _(c):
        part = pl.ds(c * BLK, BLK)
        fields = lax.dot_general(pick, ms[part, :].astype(bf16), NT, preferred_element_type=f32).astype(i32) - 1
        cu, cv, tu, tv = (fields[i:i + 1] for i in range(4))
        ku = dot(table_tr, (phase_ids == tu).astype(f32).astype(bf16))
        kv = dot(table_tr, (phase_ids == tv).astype(f32).astype(bf16))
        off = u_ids - (cu + 4)
        weights = jnp.zeros((EU, BLK), f32)
        for a in range(TAPS):
            weights = jnp.where(off == a, ku[a:a + 1], weights)
        wu[c] = weights.astype(bf16)
        taps_v[c, 0:8] = kv
        taps_v[c, 8:16] = jnp.broadcast_to(cv, (8, BLK)).astype(f32)

    @pl.loop(0, chunks)
    def _(c):
        v_first = 2 * span_s[0, c]
        steps = 2 * (span_s[1, c] - span_s[0, c]) + TAPS + 1

        @pl.loop(0, (steps + GROUP - 1) // GROUP)
        def _(g):
            x = xs[pl.ds(c * BLK, BLK), :].astype(bf16)
            v_at = v_first + g * GROUP
            off_v = (t_ids + v_at) - taps_v[c, 8:9].astype(i32)
            wv = jnp.zeros((GROUP + 4, BLK), f32)
            for a in range(TAPS):
                wv = jnp.where(off_v == a, taps_v[c, a:a + 1], wv)
            wv = wv.T.astype(bf16)
            for j in range(0, GROUP, 2):
                rhs = jnp.concatenate([x * wv[:, j:j + 1], x * wv[:, j + 1:j + 2]], 1)
                add = dot(wu[c], rhs)
                for i in range(2):
                    at = pl.ds((v_at + j + i) * EU, EU)
                    grid[at, :] = grid[at, :] + add[:, i * FEAT:(i + 1) * FEAT]

    def out_copy(u):
        return pltpu.make_async_copy(grid3.at[pl.ds(PAD, TV), 8 + u], out_hbm.at[u], out_sems.at[0])

    @pl.loop(0, TU)
    def _(u):
        out_copy(u).start()

    ve_low[...] = grid[pl.ds(0, PAD * EU), :].astype(bf16)
    ve_high[...] = grid[pl.ds((TV + PAD) * EU, PAD * EU), :].astype(bf16)

    def edge_copy(e, u):
        at = (PAD, TU + 8)[e] + u
        return pltpu.make_async_copy(grid3.at[pl.ds(PAD, TV), at], ue_ref.at[e, u], out_sems.at[1])

    for e in range(2):
        for u in range(PAD):
            edge_copy(e, u).start()
    for e in range(2):
        for u in range(PAD):
            edge_copy(e, u).wait()

    @pl.loop(0, TU)
    def _(u):
        out_copy(u).wait()


def grid_rows(recv, table):
    sources = recv.shape[0]
    slots = sources * CAP
    vmem = pl.BlockSpec(memory_space=pltpu.VMEM)
    return pl.pallas_call(
        grid_kernel,
        in_specs=[vmem, vmem],
        out_specs=(pl.BlockSpec(memory_space=pl.ANY), vmem, vmem, vmem),
        out_shape=(
            jax.ShapeDtypeStruct((TU, TV, FEAT), f32),
            jax.ShapeDtypeStruct((PAD * EU, FEAT), bf16),
            jax.ShapeDtypeStruct((PAD * EU, FEAT), bf16),
            jax.ShapeDtypeStruct((2, PAD, TV, FEAT), f32),
        ),
        scratch_shapes=[
            pltpu.VMEM((slots, FEAT), f32),
            pltpu.VMEM((slots, FEAT), f32),
            pltpu.VMEM((slots, FEAT), f32),
            pltpu.VMEM((slots, FEAT), f32),
            pltpu.VMEM((sources, FEAT), f32),
            pltpu.VMEM((FEAT, sources), f32),
            pltpu.VMEM((slots // BLK, BLK), i32),
            pltpu.SMEM((slots // BLK, BLK), i32),
            pltpu.VMEM((8, 128), i32),
            pltpu.SMEM((8, 128), i32),
            pltpu.VMEM((slots // BLK, EU, BLK), bf16),
            pltpu.VMEM((slots // BLK, 16, BLK), f32),
            pltpu.VMEM((EV, EU, FEAT), f32),
            pltpu.SemaphoreType.DMA((2,)),
            pltpu.SemaphoreType.DMA((2,)),
        ],
        compiler_params=pltpu.CompilerParams(vmem_limit_bytes=36 * MIB),
        name="grid_rows",
    )(recv, table)


def corner_kernel(low_ref, high_ref, ue_ref, send_low, send_high, low, high, edges):
    edges[...] = ue_ref[...]
    low[...] = low_ref[...].astype(f32)
    high[...] = high_ref[...].astype(f32)
    for e, (at, send) in enumerate(((PAD, send_low), (TU + 8, send_high))):
        for u in range(PAD):
            there = pl.ds(at + u, PAD, stride=EU)
            edges[e, u, 0:PAD, :] += low[there, :]
            edges[e, u, TV - PAD:TV, :] += high[there, :]
        send[...] = edges[e].astype(bf16)


def add_corners(low, high, ue):
    edge = jax.ShapeDtypeStruct(ue.shape[1:], bf16)
    return pl.pallas_call(
        corner_kernel,
        out_shape=(edge, edge),
        scratch_shapes=[
            pltpu.VMEM(low.shape, f32),
            pltpu.VMEM(high.shape, f32),
            pltpu.VMEM(ue.shape, f32),
        ],
        compiler_params=pltpu.CompilerParams(vmem_limit_bytes=8 * MIB),
        name="add_corners",
    )(low, high, ue)


def v_edge_kernel(out_in, low_ref, high_ref, out_hbm, own_ref, low, high, edges, sems):
    def copy(e, back):
        there = out_hbm.at[:, pl.ds(e * (TV - 8), 8)]
        ends = (edges.at[e], there) if back else (there, edges.at[e])
        return pltpu.make_async_copy(*ends, sems.at[e])

    copy(0, False).start()
    copy(1, False).start()
    low[...] = low_ref[...].astype(f32)
    high[...] = high_ref[...].astype(f32)
    for e, (halo, at) in enumerate(((low, 0), (high, 8 - PAD))):
        copy(e, False).wait()

        @pl.loop(0, TU // 8)
        def _(t):
            for j in range(8):
                u = t * 8 + j
                edges[e, u, at:at + PAD, :] += halo[pl.ds(8 + u, PAD, stride=EU), :]

        copy(e, True).start()
    copy(0, True).wait()
    copy(1, True).wait()
    own = [
        pltpu.make_async_copy(out_hbm.at[pl.ds(e * (TU - PAD), PAD)], own_ref.at[e], sems.at[e])
        for e in range(2)
    ]
    own[0].start()
    own[1].start()
    own[0].wait()
    own[1].wait()


def add_v_edges(out, low, high):
    vmem = pl.BlockSpec(memory_space=pltpu.VMEM)
    hbm = pl.BlockSpec(memory_space=pl.ANY)
    return pl.pallas_call(
        v_edge_kernel,
        in_specs=[hbm, vmem, vmem],
        out_specs=(hbm, vmem),
        out_shape=(
            jax.ShapeDtypeStruct(out.shape, f32),
            jax.ShapeDtypeStruct((2, PAD, TV, FEAT), f32),
        ),
        scratch_shapes=[
            pltpu.VMEM(low.shape, f32),
            pltpu.VMEM(high.shape, f32),
            pltpu.VMEM((2, TU, 8, FEAT), f32),
            pltpu.SemaphoreType.DMA((2,)),
        ],
        input_output_aliases={0: 0},
        compiler_params=pltpu.CompilerParams(vmem_limit_bytes=8 * MIB),
        name="add_v_edges",
    )(out, low, high)


def u_edge_kernel(out_in, low_ref, high_ref, own_ref, out_hbm, edges, sems):
    def copy(e):
        return pltpu.make_async_copy(edges.at[e], out_hbm.at[pl.ds(e * (TU - PAD), PAD)], sems.at[e])

    edges[0] = own_ref[0] + low_ref[...].astype(f32)
    copy(0).start()
    edges[1] = own_ref[1] + high_ref[...].astype(f32)
    copy(1).start()
    copy(0).wait()
    copy(1).wait()


def add_u_edges(out, low, high, own):
    vmem = pl.BlockSpec(memory_space=pltpu.VMEM)
    hbm = pl.BlockSpec(memory_space=pl.ANY)
    return pl.pallas_call(
        u_edge_kernel,
        in_specs=[hbm, vmem, vmem, vmem],
        out_specs=hbm,
        out_shape=jax.ShapeDtypeStruct(out.shape, f32),
        scratch_shapes=[pltpu.VMEM(own.shape, f32), pltpu.SemaphoreType.DMA((2,))],
        input_output_aliases={0: 0},
        compiler_params=pltpu.CompilerParams(vmem_limit_bytes=8 * MIB),
        name="add_u_edges",
    )(out, low, high, own)


def shifted(x, axis, up):
    n = lax.axis_size(axis)
    pairs = [(i, i + 1) if up else (i + 1, i) for i in range(n - 1)]
    return lax.ppermute(x, axis, pairs)


def local(visibility, destination, cell_u, cell_v, tap_u, tap_v, kernel_table):
    axes = ("au", "vert")
    tiles = lax.axis_size("au") * lax.axis_size("vert")
    sent = pack(visibility, destination, cell_u, cell_v, tap_u, tap_v, tiles)
    recv = lax.all_to_all(sent, axes, split_axis=0, concat_axis=0, tiled=True)
    out, ve_low, ve_high, ue = grid_rows(recv, kernel_table.T)
    v_low = shifted(ve_high, "vert", True)
    v_high = shifted(ve_low, "vert", False)
    send_low, send_high = add_corners(v_low, v_high, ue)
    u_low = shifted(send_high, "au", True)
    u_high = shifted(send_low, "au", False)
    out, own = add_v_edges(out, v_low, v_high)
    return add_u_edges(out, u_low, u_high, own)


def solution(mesh):
    rows = P(("au", "vert"))
    return jax.shard_map(
        local,
        mesh=mesh,
        in_specs=(P(("au", "vert"), None), P(("au", "vert"), None), rows, rows, rows, rows, P()),
        out_specs=P("au", "vert", None),
        check_vma=False,
    )
```

```python
import jax
import jax.numpy as jnp
from jax import lax
from jax.experimental import pallas as pl
from jax.experimental.pallas import tpu as pltpu
from jax.sharding import PartitionSpec as P

FEAT = 128
TAPS = 8
TU = 128
TV = 128
CAP = 32
SENT = CAP + 8
BLK = 256
EU = 144
EV = 160
PAD = 4
GROUP = 20
MIB = 1024 * 1024
NT = (((1,), (1,)), ((), ()))

f32 = jnp.float32
bf16 = jnp.bfloat16
i32 = jnp.int32


def iota(shape, dim):
    return lax.broadcasted_iota(i32, shape, dim)


def dot(a, b):
    return jnp.dot(a, b, preferred_element_type=f32)


def earlier(n):
    return (iota((n, n), 0) < iota((n, n), 1)).astype(f32).astype(bf16)


def pack_kernel(
    dest_hbm, cu_hbm, cv_hbm, tu_hbm, tv_hbm, vis_hbm, out_ref,
    dest_ref, cu_ref, cv_ref, tu_ref, tv_ref, vis_ref, slot_v, slot_s, xf, packed, meta, sems,
):
    rows = vis_ref.shape[0]
    ins = [
        pltpu.make_async_copy(there, here, sems.at[i])
        for i, (there, here) in enumerate((
            (dest_hbm, dest_ref), (cu_hbm, cu_ref), (cv_hbm, cv_ref),
            (tu_hbm, tu_ref), (tv_hbm, tv_ref), (vis_hbm, vis_ref),
        ))
    ]
    for copy in ins:
        copy.start()
    tiles = out_ref.shape[0]
    blocks = rows // BLK
    before = earlier(BLK)
    base = jnp.zeros((tiles, 1), f32)
    placed = jnp.zeros((tiles, 4 * CAP), f32)

    @pl.loop(0, tiles)
    def _(t):
        packed[pl.ds(t * CAP, CAP), :] = jnp.zeros((CAP, FEAT), f32)

    for copy in ins[:5]:
        copy.wait()
    tile_ids = iota((tiles, BLK), 0)
    cap_ids = iota((CAP, BLK), 0)
    for b in range(blocks):
        part = pl.ds(b * BLK, BLK)
        d = dest_ref[:, part]
        mine = (tile_ids == d).astype(f32)
        mine16 = mine.astype(bf16)
        rank = jnp.sum(mine * (dot(mine16, before) + base), 0, keepdims=True).astype(i32)
        base = base + jnp.sum(mine, 1, keepdims=True)
        slot_v[pl.ds(b, 1), :] = d * CAP + rank
        at = cap_ids == rank
        fields = [
            jnp.where(at, (ref[:, part] + 1).astype(f32), 0.0)
            for ref in (cu_ref, cv_ref, tu_ref, tv_ref)
        ]
        fields = jnp.concatenate(fields, 0).astype(bf16)
        placed = placed + lax.dot_general(mine16, fields, NT, preferred_element_type=f32)
    meta[...] = placed
    copy = pltpu.make_async_copy(slot_v, slot_s, sems.at[6])
    copy.start()
    ins[5].wait()

    @pl.loop(0, rows // 32)
    def _(t):
        part = pl.ds(t * 32, 32)
        xf[part, :] = vis_ref[part, :].astype(f32)

    copy.wait()
    step = 32

    for b in range(blocks):

        @pl.loop(0, BLK // step)
        def _(t):
            for j in range(step):
                at = t * step + j
                packed[pl.ds(slot_s[b, at], 1), :] = xf[pl.ds(b * BLK + at, 1), :]

    @pl.loop(0, tiles)
    def _(t):
        rows_t = packed[pl.ds(t * CAP, CAP), :]
        meta_t = jnp.broadcast_to(meta[pl.ds(t, 1), :], (SENT - CAP, FEAT))
        out_ref[t] = jnp.concatenate([rows_t, meta_t], 0).astype(bf16)


def pack(visibility, destination, cell_u, cell_v, tap_u, tap_v, tiles):
    rows = visibility.shape[0]
    row = lambda x: x.reshape(1, rows)
    return pl.pallas_call(
        pack_kernel,
        in_specs=[pl.BlockSpec(memory_space=pltpu.HBM)] * 6,
        out_shape=jax.ShapeDtypeStruct((tiles, SENT, FEAT), bf16),
        scratch_shapes=[pltpu.VMEM((1, rows), i32)] * 5 + [
            pltpu.VMEM((rows, FEAT), bf16),
            pltpu.VMEM((rows // BLK, BLK), i32),
            pltpu.SMEM((rows // BLK, BLK), i32),
            pltpu.VMEM((rows, FEAT), f32),
            pltpu.VMEM((tiles * CAP, FEAT), f32),
            pltpu.VMEM((tiles, FEAT), f32),
            pltpu.SemaphoreType.DMA((7,)),
        ],
        compiler_params=pltpu.CompilerParams(vmem_limit_bytes=60 * MIB),
        name="pack_rows",
    )(row(destination), row(cell_u), row(cell_v), row(tap_u), row(tap_v), visibility)


def grid_kernel(
    recv_ref, table_hbm, out_hbm, ve_low, ve_high, ue_ref,
    xf, xm, xs, ms, meta, meta_t, pos_v, pos_s, span_v, span_s,
    wu_a, wu_b, taps_a, taps_b, xt_a, xt_b, wv_a, wv_b, table_ref, grid3, sems, out_sems,
):
    grid = grid3.reshape(EV * EU, FEAT)
    sources = recv_ref.shape[0]
    slots = sources * CAP
    blocks = slots // BLK
    lanes = BLK // sources

    @pl.loop(0, sources)
    def _(s):
        x = recv_ref[s].astype(f32)
        xf[pl.ds(s * CAP, CAP), :] = x[:CAP]
        meta[pl.ds(s, 1), :] = x[CAP:CAP + 1]

    table_copy = pltpu.make_async_copy(table_hbm, table_ref, sems.at[2])
    table_copy.start()
    placed = meta[...]
    meta_t[...] = placed.T
    keys = 64

    def key_row(b):
        out = []
        for k in range(b * lanes, (b + 1) * lanes):
            cu1 = meta_t[pl.ds(k, 1), :].astype(i32)
            cv1 = meta_t[pl.ds(CAP + k, 1), :].astype(i32)
            out.append(jnp.where(cu1 > 0, (cv1 - 1) >> 1, keys))
        return jnp.concatenate(out, 1)

    key_ids = iota((128, BLK), 0)
    total = jnp.zeros((128, BLK), f32)
    for b in range(blocks):
        total = total + (key_ids == key_row(b)).astype(f32)
    total = jnp.broadcast_to(jnp.sum(total, 1, keepdims=True), (128, 128))
    below = (iota((128, 128), 1) < iota((128, 128), 0)).astype(f32).astype(bf16)
    high = jnp.floor(total * (1.0 / 64.0))
    low = total - 64.0 * high
    start = 64.0 * dot(below, high.astype(bf16)) + dot(below, low.astype(bf16))
    count = start[keys:keys + 1, :]
    lane = iota((128, 128), 1).astype(f32) * BLK
    real = iota((128, 128), 0) < keys
    first = jnp.sum(jnp.where(real & (start + total <= lane), 1.0, 0.0), 0, keepdims=True)
    last = jnp.sum(jnp.where(real & (start < jnp.minimum(lane + BLK, count)), 1.0, 0.0), 0, keepdims=True) - 1.0
    span_v[...] = jnp.concatenate([first, last, count, jnp.zeros((5, 128), f32)], 0).astype(i32)
    span_copy = pltpu.make_async_copy(span_v, span_s, sems.at[0])
    span_copy.start()
    before = earlier(BLK)
    base = start[:, 0:1]
    for b in range(blocks):
        mine = (key_ids == key_row(b)).astype(f32)
        pos = jnp.sum(mine * (dot(mine.astype(bf16), before) + base), 0, keepdims=True)
        pos_v[pl.ds(b, 1), :] = pos.astype(i32)
        base = base + jnp.sum(mine, 1, keepdims=True)
    pos_copy = pltpu.make_async_copy(pos_v, pos_s, sems.at[1])
    pos_copy.start()
    for k in range(CAP):
        xm[pl.ds(k * sources, sources), :] = pltpu.roll(placed, (FEAT - k) % FEAT, 1)

    @pl.loop(0, EV)
    def _(t):
        grid[pl.ds(t * EU, EU), :] = jnp.zeros((EU, FEAT), f32)

    table_copy.wait()
    pos_copy.wait()
    span_copy.wait()

    @pl.loop(0, sources)
    def _(s):
        for k in range(CAP):
            p = pos_s[k // lanes, (k % lanes) * sources + s]
            xs[pl.ds(p, 1), :] = xf[pl.ds(s * CAP + k, 1), :]
            ms[pl.ds(p, 1), :] = xm[pl.ds(k * sources + s, 1), :]

    table_tr = table_ref[...]
    pick = (iota((8, FEAT), 1) == CAP * iota((8, FEAT), 0)).astype(f32).astype(bf16)
    phase_ids = iota((128, BLK), 0)
    u_ids = iota((EU, BLK), 0)
    t_ids = iota((GROUP + 4, BLK), 0)
    chunks = (span_s[2, 0] + BLK - 1) // BLK
    sets = ((wu_a, taps_a, xt_a, wv_a), (wu_b, taps_b, xt_b, wv_b))

    def v_weights(taps, v_at):
        off = (t_ids + v_at) - taps[8:9].astype(i32)
        wv = jnp.zeros((GROUP + 4, BLK), f32)
        for a in range(TAPS):
            wv = jnp.where(off == a, taps[a:a + 1], wv)
        return wv.astype(bf16)

    def prepare(c, into):
        wu, taps, xt, wv = into
        part = pl.ds(c * BLK, BLK)
        xt[...] = xs[part, :].T.astype(bf16)
        fields = lax.dot_general(pick, ms[part, :].astype(bf16), NT, preferred_element_type=f32).astype(i32) - 1
        cu, cv, tu, tv = (fields[i:i + 1] for i in range(4))
        ku = dot(table_tr, (phase_ids == tu).astype(f32).astype(bf16))
        kv = dot(table_tr, (phase_ids == tv).astype(f32).astype(bf16))
        off = u_ids - (cu + 4)
        weights = jnp.zeros((EU, BLK), f32)
        for a in range(TAPS):
            weights = jnp.where(off == a, ku[a:a + 1], weights)
        wu[...] = weights.astype(bf16)
        all_taps = jnp.concatenate([kv, jnp.broadcast_to(cv, (8, BLK)).astype(f32)], 0)
        taps[...] = all_taps
        wv[...] = v_weights(all_taps, 2 * span_s[0, c])

    def add_cells(v_at, wu, xt, wv):
        for j in range(0, GROUP, 2):
            rhs = jnp.concatenate([xt[...] * wv[i:i + 1] for i in (j, j + 1)], 0)
            add = lax.dot_general(wu[...], rhs, NT, preferred_element_type=f32)
            for i in range(2):
                at = pl.ds((v_at + j + i) * EU, EU)
                grid[at, :] = grid[at, :] + add[:, i * FEAT:(i + 1) * FEAT]

    prepare(0, sets[0])

    @pl.loop(0, (chunks + 1) // 2)
    def _(pair):
        for half in range(2):
            c = 2 * pair + half
            wu, taps, xt, wv = sets[half]
            v_first = 2 * span_s[0, c]
            steps = 2 * (span_s[1, c] - span_s[0, c]) + TAPS + 1
            prepare(jnp.minimum(c + 1, slots // BLK - 1), sets[1 - half])
            add_cells(v_first, wu, xt, wv[...])

            @pl.loop(1, (steps + GROUP - 1) // GROUP)
            def _(g):
                v_at = v_first + g * GROUP
                add_cells(v_at, wu, xt, v_weights(taps[...], v_at))

    def out_copy(u):
        return pltpu.make_async_copy(grid3.at[pl.ds(PAD, TV), 8 + u], out_hbm.at[u], out_sems.at[0])

    @pl.loop(0, TU)
    def _(u):
        out_copy(u).start()

    ve_low[...] = grid[pl.ds(0, PAD * EU), :].astype(bf16)
    ve_high[...] = grid[pl.ds((TV + PAD) * EU, PAD * EU), :].astype(bf16)

    def edge_copy(e, u):
        at = (PAD, TU + 8)[e] + u
        return pltpu.make_async_copy(grid3.at[pl.ds(PAD, TV), at], ue_ref.at[e, u], out_sems.at[1])

    for e in range(2):
        for u in range(PAD):
            edge_copy(e, u).start()
    for e in range(2):
        for u in range(PAD):
            edge_copy(e, u).wait()

    @pl.loop(0, TU)
    def _(u):
        out_copy(u).wait()


def grid_rows(recv, table):
    sources = recv.shape[0]
    slots = sources * CAP
    vmem = pl.BlockSpec(memory_space=pltpu.VMEM)
    return pl.pallas_call(
        grid_kernel,
        in_specs=[vmem, pl.BlockSpec(memory_space=pltpu.HBM)],
        out_specs=(pl.BlockSpec(memory_space=pltpu.HBM), vmem, vmem, vmem),
        out_shape=(
            jax.ShapeDtypeStruct((TU, TV, FEAT), f32),
            jax.ShapeDtypeStruct((PAD * EU, FEAT), bf16),
            jax.ShapeDtypeStruct((PAD * EU, FEAT), bf16),
            jax.ShapeDtypeStruct((2, PAD, TV, FEAT), f32),
        ),
        scratch_shapes=[
            pltpu.VMEM((slots, FEAT), f32),
            pltpu.VMEM((slots, FEAT), f32),
            pltpu.VMEM((slots, FEAT), f32),
            pltpu.VMEM((slots, FEAT), f32),
            pltpu.VMEM((sources, FEAT), f32),
            pltpu.VMEM((FEAT, sources), f32),
            pltpu.VMEM((slots // BLK, BLK), i32),
            pltpu.SMEM((slots // BLK, BLK), i32),
            pltpu.VMEM((8, 128), i32),
            pltpu.SMEM((8, 128), i32),
            pltpu.VMEM((EU, BLK), bf16),
            pltpu.VMEM((EU, BLK), bf16),
            pltpu.VMEM((16, BLK), f32),
            pltpu.VMEM((16, BLK), f32),
            pltpu.VMEM((FEAT, BLK), bf16),
            pltpu.VMEM((FEAT, BLK), bf16),
            pltpu.VMEM((GROUP + 4, BLK), bf16),
            pltpu.VMEM((GROUP + 4, BLK), bf16),
            pltpu.VMEM((TAPS, 128), bf16),
            pltpu.VMEM((EV, EU, FEAT), f32),
            pltpu.SemaphoreType.DMA((3,)),
            pltpu.SemaphoreType.DMA((2,)),
        ],
        compiler_params=pltpu.CompilerParams(vmem_limit_bytes=48 * MIB),
        name="grid_rows",
    )(recv, table)


def corner_kernel(low_ref, high_ref, ue_ref, send_low, send_high, low, high, edges):
    edges[...] = ue_ref[...]
    low[...] = low_ref[...].astype(f32)
    high[...] = high_ref[...].astype(f32)
    for e, (at, send) in enumerate(((PAD, send_low), (TU + 8, send_high))):
        for u in range(PAD):
            there = pl.ds(at + u, PAD, stride=EU)
            edges[e, u, 0:PAD, :] += low[there, :]
            edges[e, u, TV - PAD:TV, :] += high[there, :]
        send[...] = edges[e].astype(bf16)


def add_corners(low, high, ue):
    edge = jax.ShapeDtypeStruct(ue.shape[1:], bf16)
    return pl.pallas_call(
        corner_kernel,
        out_shape=(edge, edge),
        scratch_shapes=[
            pltpu.VMEM(low.shape, f32),
            pltpu.VMEM(high.shape, f32),
            pltpu.VMEM(ue.shape, f32),
        ],
        compiler_params=pltpu.CompilerParams(vmem_limit_bytes=8 * MIB),
        name="add_corners",
    )(low, high, ue)


def v_edge_kernel(out_in, low_ref, high_ref, out_hbm, own_ref, low, high, edges, sems):
    def copy(e, back):
        there = out_hbm.at[:, pl.ds(e * (TV - 8), 8)]
        ends = (edges.at[e], there) if back else (there, edges.at[e])
        return pltpu.make_async_copy(*ends, sems.at[e])

    copy(0, False).start()
    copy(1, False).start()
    low[...] = low_ref[...].astype(f32)
    high[...] = high_ref[...].astype(f32)
    for e, (halo, at) in enumerate(((low, 0), (high, 8 - PAD))):
        copy(e, False).wait()

        @pl.loop(0, TU // 8)
        def _(t):
            for j in range(8):
                u = t * 8 + j
                edges[e, u, at:at + PAD, :] += halo[pl.ds(8 + u, PAD, stride=EU), :]

        copy(e, True).start()
    copy(0, True).wait()
    copy(1, True).wait()
    own = [
        pltpu.make_async_copy(out_hbm.at[pl.ds(e * (TU - PAD), PAD)], own_ref.at[e], sems.at[e])
        for e in range(2)
    ]
    own[0].start()
    own[1].start()
    own[0].wait()
    own[1].wait()


def add_v_edges(out, low, high):
    vmem = pl.BlockSpec(memory_space=pltpu.VMEM)
    hbm = pl.BlockSpec(memory_space=pl.ANY)
    return pl.pallas_call(
        v_edge_kernel,
        in_specs=[hbm, vmem, vmem],
        out_specs=(hbm, vmem),
        out_shape=(
            jax.ShapeDtypeStruct(out.shape, f32),
            jax.ShapeDtypeStruct((2, PAD, TV, FEAT), f32),
        ),
        scratch_shapes=[
            pltpu.VMEM(low.shape, f32),
            pltpu.VMEM(high.shape, f32),
            pltpu.VMEM((2, TU, 8, FEAT), f32),
            pltpu.SemaphoreType.DMA((2,)),
        ],
        input_output_aliases={0: 0},
        compiler_params=pltpu.CompilerParams(vmem_limit_bytes=8 * MIB),
        name="add_v_edges",
    )(out, low, high)


def u_edge_kernel(out_in, low_ref, high_ref, own_ref, out_hbm, edges, sems):
    def copy(e):
        return pltpu.make_async_copy(edges.at[e], out_hbm.at[pl.ds(e * (TU - PAD), PAD)], sems.at[e])

    edges[0] = own_ref[0] + low_ref[...].astype(f32)
    copy(0).start()
    edges[1] = own_ref[1] + high_ref[...].astype(f32)
    copy(1).start()
    copy(0).wait()
    copy(1).wait()


def add_u_edges(out, low, high, own):
    vmem = pl.BlockSpec(memory_space=pltpu.VMEM)
    hbm = pl.BlockSpec(memory_space=pl.ANY)
    return pl.pallas_call(
        u_edge_kernel,
        in_specs=[hbm, vmem, vmem, vmem],
        out_specs=hbm,
        out_shape=jax.ShapeDtypeStruct(out.shape, f32),
        scratch_shapes=[pltpu.VMEM(own.shape, f32), pltpu.SemaphoreType.DMA((2,))],
        input_output_aliases={0: 0},
        compiler_params=pltpu.CompilerParams(vmem_limit_bytes=8 * MIB),
        name="add_u_edges",
    )(out, low, high, own)


def shifted(x, axis, up):
    n = lax.axis_size(axis)
    pairs = [(i, i + 1) if up else (i + 1, i) for i in range(n - 1)]
    return lax.ppermute(x, axis, pairs)


def local(visibility, destination, cell_u, cell_v, tap_u, tap_v, kernel_table):
    axes = ("au", "vert")
    tiles = lax.axis_size("au") * lax.axis_size("vert")
    sent = pack(visibility, destination, cell_u, cell_v, tap_u, tap_v, tiles)
    recv = lax.all_to_all(sent, axes, split_axis=0, concat_axis=0, tiled=True)
    out, ve_low, ve_high, ue = grid_rows(recv, kernel_table.T)
    v_low = shifted(ve_high, "vert", True)
    v_high = shifted(ve_low, "vert", False)
    send_low, send_high = add_corners(v_low, v_high, ue)
    u_low = shifted(send_high, "au", True)
    u_high = shifted(send_low, "au", False)
    out, own = add_v_edges(out, v_low, v_high)
    return add_u_edges(out, u_low, u_high, own)


def solution(mesh):
    rows = P(("au", "vert"))
    return jax.shard_map(
        local,
        mesh=mesh,
        in_specs=(P(("au", "vert"), None), P(("au", "vert"), None), rows, rows, rows, rows, P()),
        out_specs=P("au", "vert", None),
        check_vma=False,
    )
```

```python
import jax
import jax.numpy as jnp
from jax import lax
from jax.experimental import pallas as pl
from jax.experimental.pallas import tpu as pltpu
from jax.sharding import PartitionSpec as P

FEAT = 128
TAPS = 8
TU = 128
TV = 128
CAP = 32
SENT = CAP + 8
BLK = 256
EU = 144
EV = 160
PAD = 4
GROUP = 20
MIB = 1024 * 1024
NT = (((1,), (1,)), ((), ()))

f32 = jnp.float32
bf16 = jnp.bfloat16
i32 = jnp.int32


def iota(shape, dim):
    return lax.broadcasted_iota(i32, shape, dim)


def dot(a, b):
    return jnp.dot(a, b, preferred_element_type=f32)


def earlier(n):
    return (iota((n, n), 0) < iota((n, n), 1)).astype(f32).astype(bf16)


def pack_kernel(
    dest_hbm, cu_hbm, cv_hbm, tu_hbm, tv_hbm, vis_hbm, out_ref,
    dest_ref, cu_ref, cv_ref, tu_ref, tv_ref, vis_ref, slot_v, slot_s, xf, packed, meta, sems,
):
    rows = vis_ref.shape[0]
    ins = [
        pltpu.make_async_copy(there, here, sems.at[i])
        for i, (there, here) in enumerate((
            (dest_hbm, dest_ref), (cu_hbm, cu_ref), (cv_hbm, cv_ref),
            (tu_hbm, tu_ref), (tv_hbm, tv_ref), (vis_hbm, vis_ref),
        ))
    ]
    for copy in ins:
        copy.start()
    tiles = out_ref.shape[0]
    blocks = rows // BLK
    before = earlier(BLK)
    base = jnp.zeros((tiles, 1), f32)
    placed = jnp.zeros((tiles, 4 * CAP), f32)

    @pl.loop(0, tiles)
    def _(t):
        packed[pl.ds(t * CAP, CAP), :] = jnp.zeros((CAP, FEAT), f32)

    for copy in ins[:5]:
        copy.wait()
    tile_ids = iota((tiles, BLK), 0)
    cap_ids = iota((CAP, BLK), 0)
    for b in range(blocks):
        part = pl.ds(b * BLK, BLK)
        d = dest_ref[:, part]
        mine = (tile_ids == d).astype(f32)
        mine16 = mine.astype(bf16)
        rank = jnp.sum(mine * (dot(mine16, before) + base), 0, keepdims=True).astype(i32)
        base = base + jnp.sum(mine, 1, keepdims=True)
        slot = d * CAP + rank
        slot_v[pl.ds(b, 1), :] = slot[:, :BLK // 2] + (slot[:, BLK // 2:] << 16)
        at = cap_ids == rank
        fields = [
            jnp.where(at, (ref[:, part] + 1).astype(f32), 0.0)
            for ref in (cu_ref, cv_ref, tu_ref, tv_ref)
        ]
        fields = jnp.concatenate(fields, 0).astype(bf16)
        placed = placed + lax.dot_general(mine16, fields, NT, preferred_element_type=f32)
    meta[...] = placed
    copy = pltpu.make_async_copy(slot_v, slot_s, sems.at[6])
    copy.start()
    ins[5].wait()

    @pl.loop(0, rows // 32)
    def _(t):
        xf[t] = vis_ref[pl.ds(t * 32, 32), :].astype(f32)

    copy.wait()
    step = 32

    for b in range(blocks):

        @pl.loop(0, BLK // (2 * step))
        def _(t):
            for j in range(step):
                two = slot_s[b, t * step + j]
                at = b * (BLK // step) + t
                packed[pl.ds(two & 0xFFFF, 1), :] = xf[at, pl.ds(j, 1), :]
                packed[pl.ds(two >> 16, 1), :] = xf[at + BLK // (2 * step), pl.ds(j, 1), :]

    @pl.loop(0, tiles)
    def _(t):
        rows_t = packed[pl.ds(t * CAP, CAP), :]
        meta_t = jnp.broadcast_to(meta[pl.ds(t, 1), :], (SENT - CAP, FEAT))
        out_ref[t] = jnp.concatenate([rows_t, meta_t], 0).astype(bf16)


def pack(visibility, destination, cell_u, cell_v, tap_u, tap_v, tiles):
    rows = visibility.shape[0]
    row = lambda x: x.reshape(1, rows)
    return pl.pallas_call(
        pack_kernel,
        in_specs=[pl.BlockSpec(memory_space=pltpu.HBM)] * 6,
        out_shape=jax.ShapeDtypeStruct((tiles, SENT, FEAT), bf16),
        scratch_shapes=[pltpu.VMEM((1, rows), i32)] * 5 + [
            pltpu.VMEM((rows, FEAT), bf16),
            pltpu.VMEM((rows // BLK, BLK // 2), i32),
            pltpu.SMEM((rows // BLK, BLK // 2), i32),
            pltpu.VMEM((rows // 32, 32, FEAT), f32),
            pltpu.VMEM((tiles * CAP, FEAT), f32),
            pltpu.VMEM((tiles, FEAT), f32),
            pltpu.SemaphoreType.DMA((7,)),
        ],
        compiler_params=pltpu.CompilerParams(vmem_limit_bytes=60 * MIB),
        name="pack_rows",
    )(row(destination), row(cell_u), row(cell_v), row(tap_u), row(tap_v), visibility)


def grid_kernel(
    recv_ref, table_hbm, out_hbm, ve_low, ve_high, ue_ref,
    xf, xm, xs, ms, meta, meta_t, pos_v, pos_s, span_v, span_s,
    wu_a, wu_b, taps_a, taps_b, xt_a, xt_b, wv_a, wv_b, table_ref, grid3, sems, out_sems,
):
    grid = grid3.reshape(EV * EU, FEAT)
    sources = recv_ref.shape[0]
    slots = sources * CAP
    blocks = slots // BLK
    lanes = BLK // sources

    @pl.loop(0, sources)
    def _(s):
        x = recv_ref[s].astype(f32)
        xf[s] = x[:CAP]
        meta[pl.ds(s, 1), :] = x[CAP:CAP + 1]

    table_copy = pltpu.make_async_copy(table_hbm, table_ref, sems.at[2])
    table_copy.start()
    placed = meta[...]
    meta_t[...] = placed.T
    keys = 64

    def key_row(b):
        out = []
        for k in range(b * lanes, (b + 1) * lanes):
            cu1 = meta_t[pl.ds(k, 1), :].astype(i32)
            cv1 = meta_t[pl.ds(CAP + k, 1), :].astype(i32)
            out.append(jnp.where(cu1 > 0, (cv1 - 1) >> 1, keys))
        return jnp.concatenate(out, 1)

    key_ids = iota((128, BLK), 0)
    total = jnp.zeros((128, BLK), f32)
    for b in range(blocks):
        total = total + (key_ids == key_row(b)).astype(f32)
    total = jnp.broadcast_to(jnp.sum(total, 1, keepdims=True), (128, 128))
    below = (iota((128, 128), 1) < iota((128, 128), 0)).astype(f32).astype(bf16)
    high = jnp.floor(total * (1.0 / 64.0))
    low = total - 64.0 * high
    start = 64.0 * dot(below, high.astype(bf16)) + dot(below, low.astype(bf16))
    count = start[keys:keys + 1, :]
    lane = iota((128, 128), 1).astype(f32) * BLK
    real = iota((128, 128), 0) < keys
    first = jnp.sum(jnp.where(real & (start + total <= lane), 1.0, 0.0), 0, keepdims=True)
    last = jnp.sum(jnp.where(real & (start < jnp.minimum(lane + BLK, count)), 1.0, 0.0), 0, keepdims=True) - 1.0
    span_v[...] = jnp.concatenate([first, last, count, jnp.zeros((5, 128), f32)], 0).astype(i32)
    span_copy = pltpu.make_async_copy(span_v, span_s, sems.at[0])
    span_copy.start()
    before = earlier(BLK)
    base = start[:, 0:1]
    for b in range(blocks):
        mine = (key_ids == key_row(b)).astype(f32)
        pos = jnp.sum(mine * (dot(mine.astype(bf16), before) + base), 0, keepdims=True)
        pos = pos.astype(i32)
        pos_v[pl.ds(b, 1), :] = pos[:, :BLK // 2] + (pos[:, BLK // 2:] << 16)
        base = base + jnp.sum(mine, 1, keepdims=True)
    pos_copy = pltpu.make_async_copy(pos_v, pos_s, sems.at[1])
    pos_copy.start()
    for k in range(CAP):
        xm[pl.ds(k * sources, sources), :] = pltpu.roll(placed, (FEAT - k) % FEAT, 1)

    @pl.loop(0, EV)
    def _(t):
        grid[pl.ds(t * EU, EU), :] = jnp.zeros((EU, FEAT), f32)

    table_copy.wait()
    pos_copy.wait()
    span_copy.wait()

    @pl.loop(0, sources)
    def _(s):
        for b in range(blocks):
            two = pos_s[b, s]
            for k, p in ((2 * b, two & 0xFFFF), (2 * b + 1, two >> 16)):
                xs[pl.ds(p, 1), :] = xf[s, pl.ds(k, 1), :]
                ms[pl.ds(p, 1), :] = xm[pl.ds(k * sources + s, 1), :]

    table_tr = table_ref[...]
    pick = (iota((8, FEAT), 1) == CAP * iota((8, FEAT), 0)).astype(f32).astype(bf16)
    phase_ids = iota((128, BLK), 0)
    u_ids = iota((EU, BLK), 0)
    t_ids = iota((GROUP + 4, BLK), 0)
    chunks = (span_s[2, 0] + BLK - 1) // BLK
    sets = ((wu_a, taps_a, xt_a, wv_a), (wu_b, taps_b, xt_b, wv_b))

    def v_weights(taps, v_at):
        off = (t_ids + v_at) - taps[8:9].astype(i32)
        wv = jnp.zeros((GROUP + 4, BLK), f32)
        for a in range(TAPS):
            wv = jnp.where(off == a, taps[a:a + 1], wv)
        return wv.astype(bf16)

    def prepare(c, into):
        wu, taps, xt, wv = into
        part = pl.ds(c * BLK, BLK)
        xt[...] = xs[part, :].T.astype(bf16)
        fields = lax.dot_general(pick, ms[part, :].astype(bf16), NT, preferred_element_type=f32).astype(i32) - 1
        cu, cv, tu, tv = (fields[i:i + 1] for i in range(4))
        ku = dot(table_tr, (phase_ids == tu).astype(f32).astype(bf16))
        kv = dot(table_tr, (phase_ids == tv).astype(f32).astype(bf16))
        off = u_ids - (cu + 4)
        weights = jnp.zeros((EU, BLK), f32)
        for a in range(TAPS):
            weights = jnp.where(off == a, ku[a:a + 1], weights)
        wu[...] = weights.astype(bf16)
        all_taps = jnp.concatenate([kv, jnp.broadcast_to(cv, (8, BLK)).astype(f32)], 0)
        taps[...] = all_taps
        wv[...] = v_weights(all_taps, 2 * span_s[0, c])

    def add_cells(v_at, wu, xt, wv):
        for j in range(0, GROUP, 2):
            rhs = jnp.concatenate([xt[...] * wv[i:i + 1] for i in (j, j + 1)], 0)
            add = lax.dot_general(wu[...], rhs, NT, preferred_element_type=f32)
            for i in range(2):
                at = pl.ds((v_at + j + i) * EU, EU)
                grid[at, :] = grid[at, :] + add[:, i * FEAT:(i + 1) * FEAT]

    prepare(0, sets[0])

    @pl.loop(0, (chunks + 1) // 2)
    def _(pair):
        for half in range(2):
            c = 2 * pair + half
            wu, taps, xt, wv = sets[half]
            v_first = 2 * span_s[0, c]
            steps = 2 * (span_s[1, c] - span_s[0, c]) + TAPS + 1
            prepare(jnp.minimum(c + 1, slots // BLK - 1), sets[1 - half])
            add_cells(v_first, wu, xt, wv[...])

            @pl.loop(1, (steps + GROUP - 1) // GROUP)
            def _(g):
                v_at = v_first + g * GROUP
                add_cells(v_at, wu, xt, v_weights(taps[...], v_at))

    def out_copy(u):
        return pltpu.make_async_copy(grid3.at[pl.ds(PAD, TV), 8 + u], out_hbm.at[u], out_sems.at[0])

    @pl.loop(0, TU)
    def _(u):
        out_copy(u).start()

    ve_low[...] = grid[pl.ds(0, PAD * EU), :].astype(bf16)
    ve_high[...] = grid[pl.ds((TV + PAD) * EU, PAD * EU), :].astype(bf16)

    def edge_copy(e, u):
        at = (PAD, TU + 8)[e] + u
        return pltpu.make_async_copy(grid3.at[pl.ds(PAD, TV), at], ue_ref.at[e, u], out_sems.at[1])

    for e in range(2):
        for u in range(PAD):
            edge_copy(e, u).start()
    for e in range(2):
        for u in range(PAD):
            edge_copy(e, u).wait()

    @pl.loop(0, TU)
    def _(u):
        out_copy(u).wait()


def grid_rows(recv, table):
    sources = recv.shape[0]
    slots = sources * CAP
    vmem = pl.BlockSpec(memory_space=pltpu.VMEM)
    return pl.pallas_call(
        grid_kernel,
        in_specs=[vmem, pl.BlockSpec(memory_space=pltpu.HBM)],
        out_specs=(pl.BlockSpec(memory_space=pltpu.HBM), vmem, vmem, vmem),
        out_shape=(
            jax.ShapeDtypeStruct((TU, TV, FEAT), f32),
            jax.ShapeDtypeStruct((PAD * EU, FEAT), bf16),
            jax.ShapeDtypeStruct((PAD * EU, FEAT), bf16),
            jax.ShapeDtypeStruct((2, PAD, TV, FEAT), f32),
        ),
        scratch_shapes=[
            pltpu.VMEM((sources, CAP, FEAT), f32),
            pltpu.VMEM((slots, FEAT), f32),
            pltpu.VMEM((slots, FEAT), f32),
            pltpu.VMEM((slots, FEAT), f32),
            pltpu.VMEM((sources, FEAT), f32),
            pltpu.VMEM((FEAT, sources), f32),
            pltpu.VMEM((slots // BLK, BLK // 2), i32),
            pltpu.SMEM((slots // BLK, BLK // 2), i32),
            pltpu.VMEM((8, 128), i32),
            pltpu.SMEM((8, 128), i32),
            pltpu.VMEM((EU, BLK), bf16),
            pltpu.VMEM((EU, BLK), bf16),
            pltpu.VMEM((16, BLK), f32),
            pltpu.VMEM((16, BLK), f32),
            pltpu.VMEM((FEAT, BLK), bf16),
            pltpu.VMEM((FEAT, BLK), bf16),
            pltpu.VMEM((GROUP + 4, BLK), bf16),
            pltpu.VMEM((GROUP + 4, BLK), bf16),
            pltpu.VMEM((TAPS, 128), bf16),
            pltpu.VMEM((EV, EU, FEAT), f32),
            pltpu.SemaphoreType.DMA((3,)),
            pltpu.SemaphoreType.DMA((2,)),
        ],
        compiler_params=pltpu.CompilerParams(vmem_limit_bytes=48 * MIB),
        name="grid_rows",
    )(recv, table)


def corner_kernel(low_ref, high_ref, ue_ref, send_low, send_high, low, high, edges):
    edges[...] = ue_ref[...]
    low[...] = low_ref[...].astype(f32)
    high[...] = high_ref[...].astype(f32)
    for e, (at, send) in enumerate(((PAD, send_low), (TU + 8, send_high))):
        for u in range(PAD):
            there = pl.ds(at + u, PAD, stride=EU)
            edges[e, u, 0:PAD, :] += low[there, :]
            edges[e, u, TV - PAD:TV, :] += high[there, :]
        send[...] = edges[e].astype(bf16)


def add_corners(low, high, ue):
    edge = jax.ShapeDtypeStruct(ue.shape[1:], bf16)
    return pl.pallas_call(
        corner_kernel,
        out_shape=(edge, edge),
        scratch_shapes=[
            pltpu.VMEM(low.shape, f32),
            pltpu.VMEM(high.shape, f32),
            pltpu.VMEM(ue.shape, f32),
        ],
        compiler_params=pltpu.CompilerParams(vmem_limit_bytes=8 * MIB),
        name="add_corners",
    )(low, high, ue)


def v_edge_kernel(out_in, low_ref, high_ref, out_hbm, own_ref, low, high, edges, sems):
    def copy(e, back):
        there = out_hbm.at[:, pl.ds(e * (TV - 8), 8)]
        ends = (edges.at[e], there) if back else (there, edges.at[e])
        return pltpu.make_async_copy(*ends, sems.at[e])

    copy(0, False).start()
    copy(1, False).start()
    low[...] = low_ref[...].astype(f32)
    high[...] = high_ref[...].astype(f32)
    for e, (halo, at) in enumerate(((low, 0), (high, 8 - PAD))):
        copy(e, False).wait()

        @pl.loop(0, TU // 8)
        def _(t):
            for j in range(8):
                u = t * 8 + j
                edges[e, u, at:at + PAD, :] += halo[pl.ds(8 + u, PAD, stride=EU), :]

        copy(e, True).start()
    copy(0, True).wait()
    copy(1, True).wait()
    own = [
        pltpu.make_async_copy(out_hbm.at[pl.ds(e * (TU - PAD), PAD)], own_ref.at[e], sems.at[e])
        for e in range(2)
    ]
    own[0].start()
    own[1].start()
    own[0].wait()
    own[1].wait()


def add_v_edges(out, low, high):
    vmem = pl.BlockSpec(memory_space=pltpu.VMEM)
    hbm = pl.BlockSpec(memory_space=pl.ANY)
    return pl.pallas_call(
        v_edge_kernel,
        in_specs=[hbm, vmem, vmem],
        out_specs=(hbm, vmem),
        out_shape=(
            jax.ShapeDtypeStruct(out.shape, f32),
            jax.ShapeDtypeStruct((2, PAD, TV, FEAT), f32),
        ),
        scratch_shapes=[
            pltpu.VMEM(low.shape, f32),
            pltpu.VMEM(high.shape, f32),
            pltpu.VMEM((2, TU, 8, FEAT), f32),
            pltpu.SemaphoreType.DMA((2,)),
        ],
        input_output_aliases={0: 0},
        compiler_params=pltpu.CompilerParams(vmem_limit_bytes=8 * MIB),
        name="add_v_edges",
    )(out, low, high)


def u_edge_kernel(out_in, low_ref, high_ref, own_ref, out_hbm, edges, sems):
    def copy(e):
        return pltpu.make_async_copy(edges.at[e], out_hbm.at[pl.ds(e * (TU - PAD), PAD)], sems.at[e])

    edges[0] = own_ref[0] + low_ref[...].astype(f32)
    copy(0).start()
    edges[1] = own_ref[1] + high_ref[...].astype(f32)
    copy(1).start()
    copy(0).wait()
    copy(1).wait()


def add_u_edges(out, low, high, own):
    vmem = pl.BlockSpec(memory_space=pltpu.VMEM)
    hbm = pl.BlockSpec(memory_space=pl.ANY)
    return pl.pallas_call(
        u_edge_kernel,
        in_specs=[hbm, vmem, vmem, vmem],
        out_specs=hbm,
        out_shape=jax.ShapeDtypeStruct(out.shape, f32),
        scratch_shapes=[pltpu.VMEM(own.shape, f32), pltpu.SemaphoreType.DMA((2,))],
        input_output_aliases={0: 0},
        compiler_params=pltpu.CompilerParams(vmem_limit_bytes=8 * MIB),
        name="add_u_edges",
    )(out, low, high, own)


def shifted(x, axis, up):
    n = lax.axis_size(axis)
    pairs = [(i, i + 1) if up else (i + 1, i) for i in range(n - 1)]
    return lax.ppermute(x, axis, pairs)


def local(visibility, destination, cell_u, cell_v, tap_u, tap_v, kernel_table):
    axes = ("au", "vert")
    tiles = lax.axis_size("au") * lax.axis_size("vert")
    sent = pack(visibility, destination, cell_u, cell_v, tap_u, tap_v, tiles)
    recv = lax.all_to_all(sent, axes, split_axis=0, concat_axis=0, tiled=True)
    out, ve_low, ve_high, ue = grid_rows(recv, kernel_table.T)
    v_low = shifted(ve_high, "vert", True)
    v_high = shifted(ve_low, "vert", False)
    send_low, send_high = add_corners(v_low, v_high, ue)
    u_low = shifted(send_high, "au", True)
    u_high = shifted(send_low, "au", False)
    out, own = add_v_edges(out, v_low, v_high)
    return add_u_edges(out, u_low, u_high, own)


def solution(mesh):
    rows = P(("au", "vert"))
    return jax.shard_map(
        local,
        mesh=mesh,
        in_specs=(P(("au", "vert"), None), P(("au", "vert"), None), rows, rows, rows, rows, P()),
        out_specs=P("au", "vert", None),
        check_vma=False,
    )
```

```python
import jax
import jax.numpy as jnp
from jax import lax
from jax.experimental import pallas as pl
from jax.experimental.pallas import tpu as pltpu
from jax.sharding import PartitionSpec as P

FEAT = 128
TAPS = 8
TU = 128
TV = 128
CAP = 32
SENT = CAP + 8
BLK = 256
EU = 144
EV = 160
PAD = 4
GROUP = 20
MIB = 1024 * 1024
NT = (((1,), (1,)), ((), ()))

f32 = jnp.float32
bf16 = jnp.bfloat16
i32 = jnp.int32


def iota(shape, dim):
    return lax.broadcasted_iota(i32, shape, dim)


def dot(a, b):
    return jnp.dot(a, b, preferred_element_type=f32)


def earlier(n):
    return (iota((n, n), 0) < iota((n, n), 1)).astype(f32).astype(bf16)


def pack_kernel(
    dest_hbm, cu_hbm, cv_hbm, tu_hbm, tv_hbm, vis_hbm, out_ref,
    dest_ref, cu_ref, cv_ref, tu_ref, tv_ref, vis_ref, slot_v, slot_s, xf, packed, meta, sems,
):
    rows = vis_ref.shape[0]
    ins = [
        pltpu.make_async_copy(there, here, sems.at[i])
        for i, (there, here) in enumerate((
            (dest_hbm, dest_ref), (cu_hbm, cu_ref), (cv_hbm, cv_ref),
            (tu_hbm, tu_ref), (tv_hbm, tv_ref), (vis_hbm, vis_ref),
        ))
    ]
    for copy in ins:
        copy.start()
    tiles = out_ref.shape[0]
    blocks = rows // BLK
    before = earlier(BLK)
    base = jnp.zeros((tiles, 1), f32)
    placed = jnp.zeros((tiles, 4 * CAP), f32)

    @pl.loop(0, tiles // 4)
    def _(t):
        packed[pl.ds(t * 4 * CAP, 4 * CAP), :] = jnp.zeros((4 * CAP, FEAT), f32)

    for copy in ins[:5]:
        copy.wait()
    tile_ids = iota((tiles, BLK), 0)
    cap_ids = iota((CAP, BLK), 0)
    for b in range(blocks):
        part = pl.ds(b * BLK, BLK)
        d = dest_ref[:, part]
        mine = (tile_ids == d).astype(f32)
        mine16 = mine.astype(bf16)
        rank = jnp.sum(mine * (dot(mine16, before) + base), 0, keepdims=True).astype(i32)
        base = base + jnp.sum(mine, 1, keepdims=True)
        slot = d * CAP + rank
        slot_v[pl.ds(b, 1), :] = slot[:, :BLK // 2] + (slot[:, BLK // 2:] << 16)
        at = cap_ids == rank
        fields = [
            jnp.where(at, (ref[:, part] + 1).astype(f32), 0.0)
            for ref in (cu_ref, cv_ref, tu_ref, tv_ref)
        ]
        fields = jnp.concatenate(fields, 0).astype(bf16)
        placed = placed + lax.dot_general(mine16, fields, NT, preferred_element_type=f32)
    meta[...] = placed
    copy = pltpu.make_async_copy(slot_v, slot_s, sems.at[6])
    copy.start()
    ins[5].wait()

    @pl.loop(0, rows // 128)
    def _(t):
        for j in range(4):
            xf[4 * t + j] = vis_ref[pl.ds(t * 128 + j * 32, 32), :].astype(f32)

    copy.wait()
    step = 32

    for b in range(blocks):

        @pl.loop(0, BLK // (2 * step))
        def _(t):
            for j in range(step):
                two = slot_s[b, t * step + j]
                at = b * (BLK // step) + t
                packed[pl.ds(two & 0xFFFF, 1), :] = xf[at, pl.ds(j, 1), :]
                packed[pl.ds(two >> 16, 1), :] = xf[at + BLK // (2 * step), pl.ds(j, 1), :]

    @pl.loop(0, tiles // 4)
    def _(group):
        for j in range(4):
            t = 4 * group + j
            rows_t = packed[pl.ds(t * CAP, CAP), :]
            meta_t = jnp.broadcast_to(meta[pl.ds(t, 1), :], (SENT - CAP, FEAT))
            out_ref[t] = jnp.concatenate([rows_t, meta_t], 0).astype(bf16)


def pack(visibility, destination, cell_u, cell_v, tap_u, tap_v, tiles):
    rows = visibility.shape[0]
    row = lambda x: x.reshape(1, rows)
    return pl.pallas_call(
        pack_kernel,
        in_specs=[pl.BlockSpec(memory_space=pltpu.HBM)] * 6,
        out_shape=jax.ShapeDtypeStruct((tiles, SENT, FEAT), bf16),
        scratch_shapes=[pltpu.VMEM((1, rows), i32)] * 5 + [
            pltpu.VMEM((rows, FEAT), bf16),
            pltpu.VMEM((rows // BLK, BLK // 2), i32),
            pltpu.SMEM((rows // BLK, BLK // 2), i32),
            pltpu.VMEM((rows // 32, 32, FEAT), f32),
            pltpu.VMEM((tiles * CAP, FEAT), f32),
            pltpu.VMEM((tiles, FEAT), f32),
            pltpu.SemaphoreType.DMA((7,)),
        ],
        compiler_params=pltpu.CompilerParams(vmem_limit_bytes=60 * MIB),
        name="pack_rows",
    )(row(destination), row(cell_u), row(cell_v), row(tap_u), row(tap_v), visibility)


def grid_kernel(
    recv_ref, table_hbm, grid3, ve_low, ve_high, ue_ref,
    xf, xs, fields_ref, meta, meta_t, pos_v, pos_s, span_v, span_s,
    wu_a, wu_b, taps_a, taps_b, xt_a, xt_b, wv_a, wv_b, table_ref, sems, out_sems,
):
    grid = grid3.reshape(EV * EU, FEAT)
    sources = recv_ref.shape[0]
    slots = sources * CAP
    blocks = slots // BLK
    lanes = BLK // sources

    @pl.loop(0, sources // 4)
    def _(t):
        for j in range(4):
            s = 4 * t + j
            x = recv_ref[s].astype(f32)
            xf[s] = x[:CAP]
            meta[pl.ds(s, 1), :] = x[CAP:CAP + 1]

    table_copy = pltpu.make_async_copy(table_hbm, table_ref, sems.at[2])
    table_copy.start()
    placed = meta[...]
    meta_t[...] = placed.T
    keys = 64

    def field_row(f, b):
        return jnp.concatenate(
            [meta_t[pl.ds(f * CAP + k, 1), :] for k in range(b * lanes, (b + 1) * lanes)], 1
        )

    def key_row(b):
        cu1 = field_row(0, b).astype(i32)
        cv1 = field_row(1, b).astype(i32)
        return jnp.where(cu1 > 0, (cv1 - 1) >> 1, keys)

    key_ids = iota((128, BLK), 0)
    total = jnp.zeros((128, BLK), f32)
    for b in range(blocks):
        total = total + (key_ids == key_row(b)).astype(f32)
    total = jnp.broadcast_to(jnp.sum(total, 1, keepdims=True), (128, 128))
    below = (iota((128, 128), 1) < iota((128, 128), 0)).astype(f32).astype(bf16)
    high = jnp.floor(total * (1.0 / 64.0))
    low = total - 64.0 * high
    start = 64.0 * dot(below, high.astype(bf16)) + dot(below, low.astype(bf16))
    count = start[keys:keys + 1, :]
    lane = iota((128, 128), 1).astype(f32) * BLK
    real = iota((128, 128), 0) < keys
    first = jnp.sum(jnp.where(real & (start + total <= lane), 1.0, 0.0), 0, keepdims=True)
    last = jnp.sum(jnp.where(real & (start < jnp.minimum(lane + BLK, count)), 1.0, 0.0), 0, keepdims=True) - 1.0
    span_v[...] = jnp.concatenate([first, last, count, jnp.zeros((5, 128), f32)], 0).astype(i32)
    span_copy = pltpu.make_async_copy(span_v, span_s, sems.at[0])
    span_copy.start()
    before = earlier(BLK)
    base = start[:, 0:1]
    pos_rows = []
    for b in range(blocks):
        mine = (key_ids == key_row(b)).astype(f32)
        pos = jnp.sum(mine * (dot(mine.astype(bf16), before) + base), 0, keepdims=True)
        pos = pos.astype(i32)
        pos_rows.append(pos)
        pos_v[pl.ds(b, 1), :] = pos[:, :BLK // 2] + (pos[:, BLK // 2:] << 16)
        base = base + jnp.sum(mine, 1, keepdims=True)
    pos_copy = pltpu.make_async_copy(pos_v, pos_s, sems.at[1])
    pos_copy.start()
    ordered = jnp.zeros((4 * blocks, BLK), f32)
    chunk_ids = iota((blocks, BLK), 0)
    place_ids = iota((BLK, BLK), 0)
    for b in range(blocks):
        chunk = chunk_ids == (pos_rows[b] >> 8)
        values = jnp.concatenate([jnp.where(chunk, field_row(f, b), 0.0) for f in range(4)], 0)
        place = (place_ids == (pos_rows[b] & (BLK - 1))).astype(f32).astype(bf16)
        ordered = ordered + lax.dot_general(values.astype(bf16), place, NT, preferred_element_type=f32)
    fields_ref[...] = ordered.astype(i32) - 1

    @pl.loop(0, EV)
    def _(t):
        grid[pl.ds(t * EU, EU), :] = jnp.zeros((EU, FEAT), f32)

    table_copy.wait()
    pos_copy.wait()
    span_copy.wait()

    @pl.loop(0, sources)
    def _(s):
        for b in range(blocks):
            two = pos_s[b, s]
            for k, p in ((2 * b, two & 0xFFFF), (2 * b + 1, two >> 16)):
                xs[pl.ds(p, 1), :] = xf[s, pl.ds(k, 1), :]

    table_tr = table_ref[...]
    phase_ids = iota((128, BLK), 0)
    u_ids = iota((EU, BLK), 0)
    t_ids = iota((GROUP + 4, BLK), 0)
    chunks = (span_s[2, 0] + BLK - 1) // BLK
    sets = ((wu_a, taps_a, xt_a, wv_a), (wu_b, taps_b, xt_b, wv_b))

    def v_weights(taps, v_at):
        off = (t_ids + v_at) - taps[8:9].astype(i32)
        wv = jnp.zeros((GROUP + 4, BLK), f32)
        for a in range(TAPS):
            wv = jnp.where(off == a, taps[a:a + 1], wv)
        return wv.astype(bf16)

    def prepare(c, into):
        wu, taps, xt, wv = into
        part = pl.ds(c * BLK, BLK)
        xt[...] = xs[part, :].T.astype(bf16)
        cu, cv, tu, tv = (fields_ref[pl.ds(f * blocks + c, 1), :] for f in range(4))
        ku = dot(table_tr, (phase_ids == tu).astype(f32).astype(bf16))
        kv = dot(table_tr, (phase_ids == tv).astype(f32).astype(bf16))
        off = u_ids - (cu + 4)
        weights = jnp.zeros((EU, BLK), f32)
        for a in range(TAPS):
            weights = jnp.where(off == a, ku[a:a + 1], weights)
        wu[...] = weights.astype(bf16)
        all_taps = jnp.concatenate([kv, jnp.broadcast_to(cv, (8, BLK)).astype(f32)], 0)
        taps[...] = all_taps
        wv[...] = v_weights(all_taps, 2 * span_s[0, c])

    def add_cells(v_at, wu, xt, wv):
        for j in range(0, GROUP, 2):
            rhs = jnp.concatenate([xt[...] * wv[i:i + 1] for i in (j, j + 1)], 0)
            add = lax.dot_general(wu[...], rhs, NT, preferred_element_type=f32)
            for i in range(2):
                at = pl.ds((v_at + j + i) * EU, EU)
                grid[at, :] = grid[at, :] + add[:, i * FEAT:(i + 1) * FEAT]

    prepare(0, sets[0])

    @pl.loop(0, (chunks + 1) // 2)
    def _(pair):
        for half in range(2):
            c = 2 * pair + half
            wu, taps, xt, wv = sets[half]
            v_first = 2 * span_s[0, c]
            steps = 2 * (span_s[1, c] - span_s[0, c]) + TAPS + 1
            prepare(jnp.minimum(c + 1, slots // BLK - 1), sets[1 - half])
            add_cells(v_first, wu, xt, wv[...])

            @pl.loop(1, (steps + GROUP - 1) // GROUP)
            def _(g):
                v_at = v_first + g * GROUP
                add_cells(v_at, wu, xt, v_weights(taps[...], v_at))

    ve_low[...] = grid[pl.ds(0, PAD * EU), :].astype(bf16)
    ve_high[...] = grid[pl.ds((TV + PAD) * EU, PAD * EU), :].astype(bf16)

    def edge_copy(e, u):
        at = (PAD, TU + 8)[e] + u
        return pltpu.make_async_copy(grid3.at[pl.ds(PAD, TV), at], ue_ref.at[e, u], out_sems.at[1])

    for e in range(2):
        for u in range(PAD):
            edge_copy(e, u).start()
    for e in range(2):
        for u in range(PAD):
            edge_copy(e, u).wait()


def grid_rows(recv, table):
    sources = recv.shape[0]
    slots = sources * CAP
    vmem = pl.BlockSpec(memory_space=pltpu.VMEM)
    return pl.pallas_call(
        grid_kernel,
        in_specs=[vmem, pl.BlockSpec(memory_space=pltpu.HBM)],
        out_specs=(vmem, vmem, vmem, vmem),
        out_shape=(
            jax.ShapeDtypeStruct((EV, EU, FEAT), f32),
            jax.ShapeDtypeStruct((PAD * EU, FEAT), bf16),
            jax.ShapeDtypeStruct((PAD * EU, FEAT), bf16),
            jax.ShapeDtypeStruct((2, PAD, TV, FEAT), f32),
        ),
        scratch_shapes=[
            pltpu.VMEM((sources, CAP, FEAT), f32),
            pltpu.VMEM((slots, FEAT), f32),
            pltpu.VMEM((4 * slots // BLK, BLK), i32),
            pltpu.VMEM((sources, FEAT), f32),
            pltpu.VMEM((FEAT, sources), f32),
            pltpu.VMEM((slots // BLK, BLK // 2), i32),
            pltpu.SMEM((slots // BLK, BLK // 2), i32),
            pltpu.VMEM((8, 128), i32),
            pltpu.SMEM((8, 128), i32),
            pltpu.VMEM((EU, BLK), bf16),
            pltpu.VMEM((EU, BLK), bf16),
            pltpu.VMEM((16, BLK), f32),
            pltpu.VMEM((16, BLK), f32),
            pltpu.VMEM((FEAT, BLK), bf16),
            pltpu.VMEM((FEAT, BLK), bf16),
            pltpu.VMEM((GROUP + 4, BLK), bf16),
            pltpu.VMEM((GROUP + 4, BLK), bf16),
            pltpu.VMEM((TAPS, 128), bf16),
            pltpu.SemaphoreType.DMA((3,)),
            pltpu.SemaphoreType.DMA((2,)),
        ],
        compiler_params=pltpu.CompilerParams(vmem_limit_bytes=24 * MIB),
        name="grid_rows",
    )(recv, table)


def corner_kernel(low_ref, high_ref, ue_ref, send_low, send_high, low, high, edges):
    edges[...] = ue_ref[...]
    low[...] = low_ref[...].astype(f32)
    high[...] = high_ref[...].astype(f32)
    for e, (at, send) in enumerate(((PAD, send_low), (TU + 8, send_high))):
        for u in range(PAD):
            there = pl.ds(at + u, PAD, stride=EU)
            edges[e, u, 0:PAD, :] += low[there, :]
            edges[e, u, TV - PAD:TV, :] += high[there, :]
        send[...] = edges[e].astype(bf16)


def add_corners(low, high, ue):
    edge = jax.ShapeDtypeStruct(ue.shape[1:], bf16)
    return pl.pallas_call(
        corner_kernel,
        out_shape=(edge, edge),
        scratch_shapes=[
            pltpu.VMEM(low.shape, f32),
            pltpu.VMEM(high.shape, f32),
            pltpu.VMEM(ue.shape, f32),
        ],
        compiler_params=pltpu.CompilerParams(vmem_limit_bytes=8 * MIB),
        name="add_corners",
    )(low, high, ue)


def tile_kernel(grid_in, low_ref, high_ref, grid3, out_hbm, own_ref, sems):
    for at, halo in ((PAD, low_ref), (TV, high_ref)):
        for v in range(PAD):
            grid3[at + v] += halo[pl.ds(v * EU, EU), :].astype(f32)

    def out_copy(u):
        return pltpu.make_async_copy(grid3.at[pl.ds(PAD, TV), 8 + u], out_hbm.at[u], sems.at[0])

    def own_copy(e, u):
        at = 8 + e * (TU - PAD) + u
        return pltpu.make_async_copy(grid3.at[pl.ds(PAD, TV), at], own_ref.at[e, u], sems.at[1])

    ends = [own_copy(e, u) for e in range(2) for u in range(PAD)]
    for copy in ends:
        copy.start()

    @pl.loop(PAD, TU - PAD)
    def _(u):
        out_copy(u).start()

    for copy in ends:
        copy.wait()

    @pl.loop(PAD, TU - PAD)
    def _(u):
        out_copy(u).wait()


def write_tile(grid, low, high):
    vmem = pl.BlockSpec(memory_space=pltpu.VMEM)
    return pl.pallas_call(
        tile_kernel,
        in_specs=[vmem] * 3,
        out_specs=(vmem, pl.BlockSpec(memory_space=pltpu.HBM), vmem),
        out_shape=(
            jax.ShapeDtypeStruct(grid.shape, f32),
            jax.ShapeDtypeStruct((TU, TV, FEAT), f32),
            jax.ShapeDtypeStruct((2, PAD, TV, FEAT), f32),
        ),
        scratch_shapes=[pltpu.SemaphoreType.DMA((2,))],
        input_output_aliases={0: 0},
        compiler_params=pltpu.CompilerParams(vmem_limit_bytes=4 * MIB),
        name="write_tile",
    )(grid, low, high)


def u_edge_kernel(out_in, low_ref, high_ref, own_ref, out_hbm, edges, sems):
    def copy(e):
        return pltpu.make_async_copy(edges.at[e], out_hbm.at[pl.ds(e * (TU - PAD), PAD)], sems.at[e])

    edges[0] = own_ref[0] + low_ref[...].astype(f32)
    copy(0).start()
    edges[1] = own_ref[1] + high_ref[...].astype(f32)
    copy(1).start()
    copy(0).wait()
    copy(1).wait()


def add_u_edges(out, low, high, own):
    vmem = pl.BlockSpec(memory_space=pltpu.VMEM)
    hbm = pl.BlockSpec(memory_space=pl.ANY)
    return pl.pallas_call(
        u_edge_kernel,
        in_specs=[hbm, vmem, vmem, vmem],
        out_specs=hbm,
        out_shape=jax.ShapeDtypeStruct(out.shape, f32),
        scratch_shapes=[pltpu.VMEM(own.shape, f32), pltpu.SemaphoreType.DMA((2,))],
        input_output_aliases={0: 0},
        compiler_params=pltpu.CompilerParams(vmem_limit_bytes=8 * MIB),
        name="add_u_edges",
    )(out, low, high, own)


def shifted(x, axis, up):
    n = lax.axis_size(axis)
    pairs = [(i, i + 1) if up else (i + 1, i) for i in range(n - 1)]
    return lax.ppermute(x, axis, pairs)


def local(visibility, destination, cell_u, cell_v, tap_u, tap_v, kernel_table):
    axes = ("au", "vert")
    tiles = lax.axis_size("au") * lax.axis_size("vert")
    sent = pack(visibility, destination, cell_u, cell_v, tap_u, tap_v, tiles)
    recv = lax.all_to_all(sent, axes, split_axis=0, concat_axis=0, tiled=True)
    grid, ve_low, ve_high, ue = grid_rows(recv, kernel_table.T)
    v_low = shifted(ve_high, "vert", True)
    v_high = shifted(ve_low, "vert", False)
    send_low, send_high = add_corners(v_low, v_high, ue)
    u_low = shifted(send_high, "au", True)
    u_high = shifted(send_low, "au", False)
    _, out, own = write_tile(grid, v_low, v_high)
    return add_u_edges(out, u_low, u_high, own)


def solution(mesh):
    rows = P(("au", "vert"))
    return jax.shard_map(
        local,
        mesh=mesh,
        in_specs=(P(("au", "vert"), None), P(("au", "vert"), None), rows, rows, rows, rows, P()),
        out_specs=P("au", "vert", None),
        check_vma=False,
    )
```

```python
import jax
import jax.numpy as jnp
from jax import lax
from jax.experimental import pallas as pl
from jax.experimental.pallas import tpu as pltpu
from jax.sharding import PartitionSpec as P

FEAT = 128
TAPS = 8
TU = 128
TV = 128
CAP = 32
SENT = CAP + 8
BLK = 256
EU = 144
EV = 160
PAD = 4
GROUP = 20
MIB = 1024 * 1024
NT = (((1,), (1,)), ((), ()))

f32 = jnp.float32
bf16 = jnp.bfloat16
i32 = jnp.int32


def iota(shape, dim):
    return lax.broadcasted_iota(i32, shape, dim)


def dot(a, b):
    return jnp.dot(a, b, preferred_element_type=f32)


def earlier(n):
    return (iota((n, n), 0) < iota((n, n), 1)).astype(f32).astype(bf16)


def pack_kernel(
    dest_hbm, cu_hbm, cv_hbm, tu_hbm, tv_hbm, vis_hbm, out_ref,
    dest_ref, cu_ref, cv_ref, tu_ref, tv_ref, vis_ref, slot_v, slot_s, xf, packed, meta, sems,
):
    rows = vis_ref.shape[0]
    ins = [
        pltpu.make_async_copy(there, here, sems.at[i])
        for i, (there, here) in enumerate((
            (dest_hbm, dest_ref), (cu_hbm, cu_ref), (cv_hbm, cv_ref),
            (tu_hbm, tu_ref), (tv_hbm, tv_ref), (vis_hbm, vis_ref),
        ))
    ]
    for copy in ins:
        copy.start()
    tiles = out_ref.shape[0]
    blocks = rows // BLK
    before = earlier(BLK)
    base = jnp.zeros((tiles, 1), f32)
    placed = jnp.zeros((tiles, 4 * CAP), f32)

    @pl.loop(0, tiles // 4)
    def _(t):
        packed[pl.ds(t * 4 * CAP, 4 * CAP), :] = jnp.zeros((4 * CAP, FEAT), f32)

    for copy in ins[:5]:
        copy.wait()
    tile_ids = iota((tiles, BLK), 0)
    cap_ids = iota((CAP, BLK), 0)
    for b in range(blocks):
        part = pl.ds(b * BLK, BLK)
        d = dest_ref[:, part]
        mine = (tile_ids == d).astype(f32)
        mine16 = mine.astype(bf16)
        rank = jnp.sum(mine * (dot(mine16, before) + base), 0, keepdims=True).astype(i32)
        base = base + jnp.sum(mine, 1, keepdims=True)
        slot = d * CAP + rank
        slot_v[pl.ds(b, 1), :] = slot[:, :BLK // 2] + (slot[:, BLK // 2:] << 16)
        at = cap_ids == rank
        fields = [
            jnp.where(at, (ref[:, part] + 1).astype(f32), 0.0)
            for ref in (cu_ref, cv_ref, tu_ref, tv_ref)
        ]
        fields = jnp.concatenate(fields, 0).astype(bf16)
        placed = placed + lax.dot_general(mine16, fields, NT, preferred_element_type=f32)
    meta[...] = placed
    copy = pltpu.make_async_copy(slot_v, slot_s, sems.at[6])
    copy.start()
    ins[5].wait()

    @pl.loop(0, rows // 128)
    def _(t):
        for j in range(4):
            xf[4 * t + j] = vis_ref[pl.ds(t * 128 + j * 32, 32), :].astype(f32)

    copy.wait()
    step = 32

    for b in range(blocks):

        @pl.loop(0, BLK // (2 * step))
        def _(t):
            for j in range(step):
                two = slot_s[b, t * step + j]
                at = b * (BLK // step) + t
                packed[pl.ds(two & 0xFFFF, 1), :] = xf[at, pl.ds(j, 1), :]
                packed[pl.ds(two >> 16, 1), :] = xf[at + BLK // (2 * step), pl.ds(j, 1), :]

    @pl.loop(0, tiles // 4)
    def _(group):
        for j in range(4):
            t = 4 * group + j
            rows_t = packed[pl.ds(t * CAP, CAP), :]
            meta_t = jnp.broadcast_to(meta[pl.ds(t, 1), :], (SENT - CAP, FEAT))
            out_ref[t] = jnp.concatenate([rows_t, meta_t], 0).astype(bf16)


def pack(visibility, destination, cell_u, cell_v, tap_u, tap_v, tiles):
    rows = visibility.shape[0]
    row = lambda x: x.reshape(1, rows)
    return pl.pallas_call(
        pack_kernel,
        in_specs=[pl.BlockSpec(memory_space=pltpu.HBM)] * 6,
        out_shape=jax.ShapeDtypeStruct((tiles, SENT, FEAT), bf16),
        scratch_shapes=[pltpu.VMEM((1, rows), i32)] * 5 + [
            pltpu.VMEM((rows, FEAT), bf16),
            pltpu.VMEM((rows // BLK, BLK // 2), i32),
            pltpu.SMEM((rows // BLK, BLK // 2), i32),
            pltpu.VMEM((rows // 32, 32, FEAT), f32),
            pltpu.VMEM((tiles * CAP, FEAT), f32),
            pltpu.VMEM((tiles, FEAT), f32),
            pltpu.SemaphoreType.DMA((7,)),
        ],
        compiler_params=pltpu.CompilerParams(vmem_limit_bytes=60 * MIB),
        name="pack_rows",
    )(row(destination), row(cell_u), row(cell_v), row(tap_u), row(tap_v), visibility)


def grid_kernel(
    recv_ref, table_hbm, grid3, ve_low, ve_high,
    xf, xs, fields_ref, meta, meta_t, pos_v, pos_s, span_v, span_s,
    wu_a, wu_b, taps_a, taps_b, xt_a, xt_b, wv_a, wv_b, table_ref, sems,
):
    grid = grid3.reshape(EV * EU, FEAT)
    sources = recv_ref.shape[0]
    slots = sources * CAP
    blocks = slots // BLK
    lanes = BLK // sources

    @pl.loop(0, sources // 4)
    def _(t):
        for j in range(4):
            s = 4 * t + j
            x = recv_ref[s].astype(f32)
            xf[s] = x[:CAP]
            meta[pl.ds(s, 1), :] = x[CAP:CAP + 1]

    table_copy = pltpu.make_async_copy(table_hbm, table_ref, sems.at[2])
    table_copy.start()
    placed = meta[...]
    meta_t[...] = placed.T
    keys = 64

    def field_row(f, b):
        return jnp.concatenate(
            [meta_t[pl.ds(f * CAP + k, 1), :] for k in range(b * lanes, (b + 1) * lanes)], 1
        )

    def key_row(b):
        cu1 = field_row(0, b).astype(i32)
        cv1 = field_row(1, b).astype(i32)
        return jnp.where(cu1 > 0, (cv1 - 1) >> 1, keys)

    key_ids = iota((128, BLK), 0)
    total = jnp.zeros((128, BLK), f32)
    for b in range(blocks):
        total = total + (key_ids == key_row(b)).astype(f32)
    total = jnp.broadcast_to(jnp.sum(total, 1, keepdims=True), (128, 128))
    below = (iota((128, 128), 1) < iota((128, 128), 0)).astype(f32).astype(bf16)
    high = jnp.floor(total * (1.0 / 64.0))
    low = total - 64.0 * high
    start = 64.0 * dot(below, high.astype(bf16)) + dot(below, low.astype(bf16))
    count = start[keys:keys + 1, :]
    lane = iota((128, 128), 1).astype(f32) * BLK
    real = iota((128, 128), 0) < keys
    first = jnp.sum(jnp.where(real & (start + total <= lane), 1.0, 0.0), 0, keepdims=True)
    last = jnp.sum(jnp.where(real & (start < jnp.minimum(lane + BLK, count)), 1.0, 0.0), 0, keepdims=True) - 1.0
    span_v[...] = jnp.concatenate([first, last, count, jnp.zeros((5, 128), f32)], 0).astype(i32)
    span_copy = pltpu.make_async_copy(span_v, span_s, sems.at[0])
    span_copy.start()
    before = earlier(BLK)
    base = start[:, 0:1]
    pos_rows = []
    for b in range(blocks):
        mine = (key_ids == key_row(b)).astype(f32)
        pos = jnp.sum(mine * (dot(mine.astype(bf16), before) + base), 0, keepdims=True)
        pos = pos.astype(i32)
        pos_rows.append(pos)
        pos_v[pl.ds(b, 1), :] = pos[:, :BLK // 2] + (pos[:, BLK // 2:] << 16)
        base = base + jnp.sum(mine, 1, keepdims=True)
    pos_copy = pltpu.make_async_copy(pos_v, pos_s, sems.at[1])
    pos_copy.start()
    ordered = jnp.zeros((4 * blocks, BLK), f32)
    chunk_ids = iota((blocks, BLK), 0)
    place_ids = iota((BLK, BLK), 0)
    for b in range(blocks):
        chunk = chunk_ids == (pos_rows[b] >> 8)
        values = jnp.concatenate([jnp.where(chunk, field_row(f, b), 0.0) for f in range(4)], 0)
        place = (place_ids == (pos_rows[b] & (BLK - 1))).astype(f32).astype(bf16)
        ordered = ordered + lax.dot_general(values.astype(bf16), place, NT, preferred_element_type=f32)
    fields_ref[...] = ordered.astype(i32) - 1

    @pl.loop(0, EV)
    def _(t):
        grid[pl.ds(t * EU, EU), :] = jnp.zeros((EU, FEAT), f32)

    table_copy.wait()
    pos_copy.wait()
    span_copy.wait()

    @pl.loop(0, sources)
    def _(s):
        for b in range(blocks):
            two = pos_s[b, s]
            for k, p in ((2 * b, two & 0xFFFF), (2 * b + 1, two >> 16)):
                xs[pl.ds(p, 1), :] = xf[s, pl.ds(k, 1), :]

    table_tr = table_ref[...]
    phase_ids = iota((128, BLK), 0)
    u_ids = iota((EU, BLK), 0)
    t_ids = iota((GROUP + 4, BLK), 0)
    chunks = (span_s[2, 0] + BLK - 1) // BLK
    sets = ((wu_a, taps_a, xt_a, wv_a), (wu_b, taps_b, xt_b, wv_b))

    def v_weights(taps, v_at):
        off = (t_ids + v_at) - taps[8:9].astype(i32)
        wv = jnp.zeros((GROUP + 4, BLK), f32)
        for a in range(TAPS):
            wv = jnp.where(off == a, taps[a:a + 1], wv)
        return wv.astype(bf16)

    def prepare(c, into):
        wu, taps, xt, wv = into
        part = pl.ds(c * BLK, BLK)
        xt[...] = xs[part, :].T.astype(bf16)
        cu, cv, tu, tv = (fields_ref[pl.ds(f * blocks + c, 1), :] for f in range(4))
        ku = dot(table_tr, (phase_ids == tu).astype(f32).astype(bf16))
        kv = dot(table_tr, (phase_ids == tv).astype(f32).astype(bf16))
        off = u_ids - (cu + 4)
        weights = jnp.zeros((EU, BLK), f32)
        for a in range(TAPS):
            weights = jnp.where(off == a, ku[a:a + 1], weights)
        wu[...] = weights.astype(bf16)
        all_taps = jnp.concatenate([kv, jnp.broadcast_to(cv, (8, BLK)).astype(f32)], 0)
        taps[...] = all_taps
        wv[...] = v_weights(all_taps, 2 * span_s[0, c])

    def add_cells(v_at, wu, xt, wv):
        for j in range(0, GROUP, 2):
            rhs = jnp.concatenate([xt[...] * wv[i:i + 1] for i in (j, j + 1)], 0)
            add = lax.dot_general(wu[...], rhs, NT, preferred_element_type=f32)
            for i in range(2):
                at = pl.ds((v_at + j + i) * EU, EU)
                grid[at, :] = grid[at, :] + add[:, i * FEAT:(i + 1) * FEAT]

    prepare(0, sets[0])

    @pl.loop(0, (chunks + 1) // 2)
    def _(pair):
        for half in range(2):
            c = 2 * pair + half
            wu, taps, xt, wv = sets[half]
            v_first = 2 * span_s[0, c]
            steps = 2 * (span_s[1, c] - span_s[0, c]) + TAPS + 1
            prepare(jnp.minimum(c + 1, slots // BLK - 1), sets[1 - half])
            add_cells(v_first, wu, xt, wv[...])

            @pl.loop(1, (steps + GROUP - 1) // GROUP)
            def _(g):
                v_at = v_first + g * GROUP
                add_cells(v_at, wu, xt, v_weights(taps[...], v_at))

    ve_low[...] = grid[pl.ds(0, PAD * EU), :].astype(bf16)
    ve_high[...] = grid[pl.ds((TV + PAD) * EU, PAD * EU), :].astype(bf16)


def grid_rows(recv, table):
    sources = recv.shape[0]
    slots = sources * CAP
    vmem = pl.BlockSpec(memory_space=pltpu.VMEM)
    return pl.pallas_call(
        grid_kernel,
        in_specs=[vmem, pl.BlockSpec(memory_space=pltpu.HBM)],
        out_specs=(vmem, vmem, vmem),
        out_shape=(
            jax.ShapeDtypeStruct((EV, EU, FEAT), f32),
            jax.ShapeDtypeStruct((PAD * EU, FEAT), bf16),
            jax.ShapeDtypeStruct((PAD * EU, FEAT), bf16),
        ),
        scratch_shapes=[
            pltpu.VMEM((sources, CAP, FEAT), f32),
            pltpu.VMEM((slots, FEAT), f32),
            pltpu.VMEM((4 * slots // BLK, BLK), i32),
            pltpu.VMEM((sources, FEAT), f32),
            pltpu.VMEM((FEAT, sources), f32),
            pltpu.VMEM((slots // BLK, BLK // 2), i32),
            pltpu.SMEM((slots // BLK, BLK // 2), i32),
            pltpu.VMEM((8, 128), i32),
            pltpu.SMEM((8, 128), i32),
            pltpu.VMEM((EU, BLK), bf16),
            pltpu.VMEM((EU, BLK), bf16),
            pltpu.VMEM((16, BLK), f32),
            pltpu.VMEM((16, BLK), f32),
            pltpu.VMEM((FEAT, BLK), bf16),
            pltpu.VMEM((FEAT, BLK), bf16),
            pltpu.VMEM((GROUP + 4, BLK), bf16),
            pltpu.VMEM((GROUP + 4, BLK), bf16),
            pltpu.VMEM((TAPS, 128), bf16),
            pltpu.SemaphoreType.DMA((3,)),
        ],
        compiler_params=pltpu.CompilerParams(vmem_limit_bytes=24 * MIB),
        name="grid_rows",
    )(recv, table)


def edge_kernel(grid3, ue_ref, sem):
    def edge_copy(e, u):
        at = (PAD, TU + 8)[e] + u
        return pltpu.make_async_copy(grid3.at[pl.ds(PAD, TV), at], ue_ref.at[e, u], sem)

    edges = [edge_copy(e, u) for e in range(2) for u in range(PAD)]
    for copy in edges:
        copy.start()
    for copy in edges:
        copy.wait()


def u_edges(grid):
    vmem = pl.BlockSpec(memory_space=pltpu.VMEM)
    return pl.pallas_call(
        edge_kernel,
        in_specs=[vmem],
        out_specs=vmem,
        out_shape=jax.ShapeDtypeStruct((2, PAD, TV, FEAT), f32),
        scratch_shapes=[pltpu.SemaphoreType.DMA(())],
        compiler_params=pltpu.CompilerParams(vmem_limit_bytes=4 * MIB),
        cost_estimate=pl.CostEstimate(flops=10**8, bytes_accessed=2 * MIB, transcendentals=0),
        name="u_edges",
    )(grid)


def corner_kernel(low_ref, high_ref, ue_ref, send_low, send_high, low, high, edges):
    edges[...] = ue_ref[...]
    low[...] = low_ref[...].astype(f32)
    high[...] = high_ref[...].astype(f32)
    for e, (at, send) in enumerate(((PAD, send_low), (TU + 8, send_high))):
        for u in range(PAD):
            there = pl.ds(at + u, PAD, stride=EU)
            edges[e, u, 0:PAD, :] += low[there, :]
            edges[e, u, TV - PAD:TV, :] += high[there, :]
        send[...] = edges[e].astype(bf16)


def add_corners(low, high, ue):
    edge = jax.ShapeDtypeStruct(ue.shape[1:], bf16)
    return pl.pallas_call(
        corner_kernel,
        out_shape=(edge, edge),
        scratch_shapes=[
            pltpu.VMEM(low.shape, f32),
            pltpu.VMEM(high.shape, f32),
            pltpu.VMEM(ue.shape, f32),
        ],
        compiler_params=pltpu.CompilerParams(vmem_limit_bytes=8 * MIB),
        name="add_corners",
    )(low, high, ue)


def tile_kernel(grid_in, low_ref, high_ref, grid3, out_hbm, own_ref, sems):
    for at, halo in ((PAD, low_ref), (TV, high_ref)):
        for v in range(PAD):
            grid3[at + v] += halo[pl.ds(v * EU, EU), :].astype(f32)

    def out_copy(u):
        return pltpu.make_async_copy(grid3.at[pl.ds(PAD, TV), 8 + u], out_hbm.at[u], sems.at[0])

    def own_copy(e, u):
        at = 8 + e * (TU - PAD) + u
        return pltpu.make_async_copy(grid3.at[pl.ds(PAD, TV), at], own_ref.at[e, u], sems.at[1])

    ends = [own_copy(e, u) for e in range(2) for u in range(PAD)]
    for copy in ends:
        copy.start()

    @pl.loop(PAD, TU - PAD)
    def _(u):
        out_copy(u).start()

    for copy in ends:
        copy.wait()

    @pl.loop(PAD, TU - PAD)
    def _(u):
        out_copy(u).wait()


def write_tile(grid, low, high):
    vmem = pl.BlockSpec(memory_space=pltpu.VMEM)
    return pl.pallas_call(
        tile_kernel,
        in_specs=[vmem] * 3,
        out_specs=(vmem, pl.BlockSpec(memory_space=pltpu.HBM), vmem),
        out_shape=(
            jax.ShapeDtypeStruct(grid.shape, f32),
            jax.ShapeDtypeStruct((TU, TV, FEAT), f32),
            jax.ShapeDtypeStruct((2, PAD, TV, FEAT), f32),
        ),
        scratch_shapes=[pltpu.SemaphoreType.DMA((2,))],
        input_output_aliases={0: 0},
        compiler_params=pltpu.CompilerParams(vmem_limit_bytes=4 * MIB),
        name="write_tile",
    )(grid, low, high)


def u_edge_kernel(out_in, low_ref, high_ref, own_ref, out_hbm, edges, sems):
    def copy(e):
        return pltpu.make_async_copy(edges.at[e], out_hbm.at[pl.ds(e * (TU - PAD), PAD)], sems.at[e])

    edges[0] = own_ref[0] + low_ref[...].astype(f32)
    copy(0).start()
    edges[1] = own_ref[1] + high_ref[...].astype(f32)
    copy(1).start()
    copy(0).wait()
    copy(1).wait()


def add_u_edges(out, low, high, own):
    vmem = pl.BlockSpec(memory_space=pltpu.VMEM)
    hbm = pl.BlockSpec(memory_space=pl.ANY)
    return pl.pallas_call(
        u_edge_kernel,
        in_specs=[hbm, vmem, vmem, vmem],
        out_specs=hbm,
        out_shape=jax.ShapeDtypeStruct(out.shape, f32),
        scratch_shapes=[pltpu.VMEM(own.shape, f32), pltpu.SemaphoreType.DMA((2,))],
        input_output_aliases={0: 0},
        compiler_params=pltpu.CompilerParams(vmem_limit_bytes=8 * MIB),
        name="add_u_edges",
    )(out, low, high, own)


def shifted(x, axis, up):
    n = lax.axis_size(axis)
    pairs = [(i, i + 1) if up else (i + 1, i) for i in range(n - 1)]
    return lax.ppermute(x, axis, pairs)


def local(visibility, destination, cell_u, cell_v, tap_u, tap_v, kernel_table):
    axes = ("au", "vert")
    tiles = lax.axis_size("au") * lax.axis_size("vert")
    sent = pack(visibility, destination, cell_u, cell_v, tap_u, tap_v, tiles)
    recv = lax.all_to_all(sent, axes, split_axis=0, concat_axis=0, tiled=True)
    grid, ve_low, ve_high = grid_rows(recv, kernel_table.T)
    v_low = shifted(ve_high, "vert", True)
    v_high = shifted(ve_low, "vert", False)
    send_low, send_high = add_corners(v_low, v_high, u_edges(grid))
    u_low = shifted(send_high, "au", True)
    u_high = shifted(send_low, "au", False)
    _, out, own = write_tile(grid, v_low, v_high)
    return add_u_edges(out, u_low, u_high, own)


def solution(mesh):
    rows = P(("au", "vert"))
    return jax.shard_map(
        local,
        mesh=mesh,
        in_specs=(P(("au", "vert"), None), P(("au", "vert"), None), rows, rows, rows, rows, P()),
        out_specs=P("au", "vert", None),
        check_vma=False,
    )
```

```python
import jax
import jax.numpy as jnp
from jax import lax
from jax.experimental import pallas as pl
from jax.experimental.pallas import tpu as pltpu
from jax.sharding import PartitionSpec as P

FEAT = 128
TAPS = 8
TU = 128
TV = 128
CAP = 32
SENT = CAP + 8
BLK = 256
EU = 144
EV = 160
PAD = 4
GROUP = 20
MIB = 1024 * 1024
NT = (((1,), (1,)), ((), ()))

f32 = jnp.float32
bf16 = jnp.bfloat16
i32 = jnp.int32


def iota(shape, dim):
    return lax.broadcasted_iota(i32, shape, dim)


def dot(a, b):
    return jnp.dot(a, b, preferred_element_type=f32)


def earlier(n):
    return (iota((n, n), 0) < iota((n, n), 1)).astype(f32).astype(bf16)


def pack_kernel(
    dest_hbm, cu_hbm, cv_hbm, tu_hbm, tv_hbm, vis_hbm, out_ref,
    dest_ref, cu_ref, cv_ref, tu_ref, tv_ref, vis_ref, slot_v, slot_s, xf, packed3, meta, sems,
):
    rows = vis_ref.shape[0]
    packed = packed3.reshape(packed3.shape[0], FEAT)
    ins = [
        pltpu.make_async_copy(there, here, sems.at[i])
        for i, (there, here) in enumerate((
            (dest_hbm, dest_ref), (cu_hbm, cu_ref), (cv_hbm, cv_ref),
            (tu_hbm, tu_ref), (tv_hbm, tv_ref), (vis_hbm, vis_ref),
        ))
    ]
    for copy in ins:
        copy.start()
    tiles = out_ref.shape[0]
    blocks = rows // BLK
    before = earlier(BLK)
    base = jnp.zeros((tiles, 1), f32)
    placed = jnp.zeros((tiles, 4 * CAP), f32)

    @pl.loop(0, tiles // 4)
    def _(t):
        packed[pl.ds(t * 4 * CAP, 4 * CAP), :] = jnp.zeros((4 * CAP, FEAT), f32)

    for copy in ins[:5]:
        copy.wait()
    tile_ids = iota((tiles, BLK), 0)
    cap_ids = iota((CAP, BLK), 0)
    for b in range(blocks):
        part = pl.ds(b * BLK, BLK)
        d = dest_ref[:, part]
        mine = (tile_ids == d).astype(f32)
        mine16 = mine.astype(bf16)
        rank = jnp.sum(mine * (dot(mine16, before) + base), 0, keepdims=True).astype(i32)
        base = base + jnp.sum(mine, 1, keepdims=True)
        slot = d * CAP + rank
        slot_v[pl.ds(b, 1), :] = slot[:, :BLK // 2] + (slot[:, BLK // 2:] << 16)
        at = cap_ids == rank
        fields = [
            jnp.where(at, (ref[:, part] + 1).astype(f32), 0.0)
            for ref in (cu_ref, cv_ref, tu_ref, tv_ref)
        ]
        fields = jnp.concatenate(fields, 0).astype(bf16)
        placed = placed + lax.dot_general(mine16, fields, NT, preferred_element_type=f32)
    meta[...] = placed
    copy = pltpu.make_async_copy(slot_v, slot_s, sems.at[6])
    copy.start()
    ins[5].wait()

    @pl.loop(0, rows // 128)
    def _(t):
        for j in range(4):
            xf[4 * t + j] = vis_ref[pl.ds(t * 128 + j * 32, 32), :].astype(f32)

    copy.wait()
    step = 32

    for b in range(blocks):

        @pl.loop(0, BLK // (2 * step))
        def _(t):
            for j in range(step):
                two = slot_s[b, t * step + j]
                at = b * (BLK // step) + t
                packed3[two & 0xFFFF] = xf[at, pl.ds(j, 1), :]
                packed3[two >> 16] = xf[at + BLK // (2 * step), pl.ds(j, 1), :]

    @pl.loop(0, tiles // 4)
    def _(group):
        for j in range(4):
            t = 4 * group + j
            rows_t = packed[pl.ds(t * CAP, CAP), :]
            meta_t = jnp.broadcast_to(meta[pl.ds(t, 1), :], (SENT - CAP, FEAT))
            out_ref[t] = jnp.concatenate([rows_t, meta_t], 0).astype(bf16)


def pack(visibility, destination, cell_u, cell_v, tap_u, tap_v, tiles):
    rows = visibility.shape[0]
    row = lambda x: x.reshape(1, rows)
    return pl.pallas_call(
        pack_kernel,
        in_specs=[pl.BlockSpec(memory_space=pltpu.HBM)] * 6,
        out_shape=jax.ShapeDtypeStruct((tiles, SENT, FEAT), bf16),
        scratch_shapes=[pltpu.VMEM((1, rows), i32)] * 5 + [
            pltpu.VMEM((rows, FEAT), bf16),
            pltpu.VMEM((rows // BLK, BLK // 2), i32),
            pltpu.SMEM((rows // BLK, BLK // 2), i32),
            pltpu.VMEM((rows // 32, 32, FEAT), f32),
            pltpu.VMEM((tiles * CAP, 1, FEAT), f32),
            pltpu.VMEM((tiles, FEAT), f32),
            pltpu.SemaphoreType.DMA((7,)),
        ],
        compiler_params=pltpu.CompilerParams(vmem_limit_bytes=60 * MIB),
        name="pack_rows",
    )(row(destination), row(cell_u), row(cell_v), row(tap_u), row(tap_v), visibility)


def grid_kernel(
    recv_ref, table_hbm, grid3, ve_low, ve_high,
    xf, xs, fields_ref, meta, meta_t, pos_v, pos_s, span_v, span_s,
    wu_a, wu_b, taps_a, taps_b, xt_a, xt_b, wv_a, wv_b, table_ref, sems,
):
    grid = grid3.reshape(EV * EU, FEAT)
    sources = recv_ref.shape[0]
    slots = sources * CAP
    blocks = slots // BLK
    lanes = BLK // sources

    @pl.loop(0, sources // 4)
    def _(t):
        for j in range(4):
            s = 4 * t + j
            x = recv_ref[s].astype(f32)
            xf[s] = x[:CAP]
            meta[pl.ds(s, 1), :] = x[CAP:CAP + 1]

    table_copy = pltpu.make_async_copy(table_hbm, table_ref, sems.at[2])
    table_copy.start()
    placed = meta[...]
    meta_t[...] = placed.T
    keys = 64

    def field_row(f, b):
        return jnp.concatenate(
            [meta_t[pl.ds(f * CAP + k, 1), :] for k in range(b * lanes, (b + 1) * lanes)], 1
        )

    def key_row(b):
        cu1 = field_row(0, b).astype(i32)
        cv1 = field_row(1, b).astype(i32)
        return jnp.where(cu1 > 0, (cv1 - 1) >> 1, keys)

    key_ids = iota((128, BLK), 0)
    total = jnp.zeros((128, BLK), f32)
    for b in range(blocks):
        total = total + (key_ids == key_row(b)).astype(f32)
    total = jnp.broadcast_to(jnp.sum(total, 1, keepdims=True), (128, 128))
    below = (iota((128, 128), 1) < iota((128, 128), 0)).astype(f32).astype(bf16)
    high = jnp.floor(total * (1.0 / 64.0))
    low = total - 64.0 * high
    start = 64.0 * dot(below, high.astype(bf16)) + dot(below, low.astype(bf16))
    count = start[keys:keys + 1, :]
    lane = iota((128, 128), 1).astype(f32) * BLK
    real = iota((128, 128), 0) < keys
    first = jnp.sum(jnp.where(real & (start + total <= lane), 1.0, 0.0), 0, keepdims=True)
    last = jnp.sum(jnp.where(real & (start < jnp.minimum(lane + BLK, count)), 1.0, 0.0), 0, keepdims=True) - 1.0
    span_v[...] = jnp.concatenate([first, last, count, jnp.zeros((5, 128), f32)], 0).astype(i32)
    span_copy = pltpu.make_async_copy(span_v, span_s, sems.at[0])
    span_copy.start()
    before = earlier(BLK)
    base = start[:, 0:1]
    pos_rows = []
    for b in range(blocks):
        mine = (key_ids == key_row(b)).astype(f32)
        pos = jnp.sum(mine * (dot(mine.astype(bf16), before) + base), 0, keepdims=True)
        pos = pos.astype(i32)
        pos_rows.append(pos)
        pos_v[pl.ds(b, 1), :] = pos[:, :BLK // 2] + (pos[:, BLK // 2:] << 16)
        base = base + jnp.sum(mine, 1, keepdims=True)
    pos_copy = pltpu.make_async_copy(pos_v, pos_s, sems.at[1])
    pos_copy.start()
    ordered = jnp.zeros((4 * blocks, BLK), f32)
    chunk_ids = iota((blocks, BLK), 0)
    place_ids = iota((BLK, BLK), 0)
    for b in range(blocks):
        chunk = chunk_ids == (pos_rows[b] >> 8)
        values = jnp.concatenate([jnp.where(chunk, field_row(f, b), 0.0) for f in range(4)], 0)
        place = (place_ids == (pos_rows[b] & (BLK - 1))).astype(f32).astype(bf16)
        ordered = ordered + lax.dot_general(values.astype(bf16), place, NT, preferred_element_type=f32)
    fields_ref[...] = ordered.astype(i32) - 1

    @pl.loop(0, EV)
    def _(t):
        grid[pl.ds(t * EU, EU), :] = jnp.zeros((EU, FEAT), f32)

    table_copy.wait()
    pos_copy.wait()
    span_copy.wait()

    @pl.loop(0, sources)
    def _(s):
        for b in range(blocks):
            two = pos_s[b, s]
            for k, p in ((2 * b, two & 0xFFFF), (2 * b + 1, two >> 16)):
                xs[pl.ds(p, 1), :] = xf[s, pl.ds(k, 1), :]

    table_tr = table_ref[...]
    phase_ids = iota((128, BLK), 0)
    u_ids = iota((EU, BLK), 0)
    t_ids = iota((GROUP + 4, BLK), 0)
    chunks = (span_s[2, 0] + BLK - 1) // BLK
    sets = ((wu_a, taps_a, xt_a, wv_a), (wu_b, taps_b, xt_b, wv_b))

    def v_weights(taps, v_at):
        off = (t_ids + v_at) - taps[8:9].astype(i32)
        wv = jnp.zeros((GROUP + 4, BLK), f32)
        for a in range(TAPS):
            wv = jnp.where(off == a, taps[a:a + 1], wv)
        return wv.astype(bf16)

    def prepare(c, into):
        wu, taps, xt, wv = into
        part = pl.ds(c * BLK, BLK)
        xt[...] = xs[part, :].T.astype(bf16)
        cu, cv, tu, tv = (fields_ref[pl.ds(f * blocks + c, 1), :] for f in range(4))
        ku = dot(table_tr, (phase_ids == tu).astype(f32).astype(bf16))
        kv = dot(table_tr, (phase_ids == tv).astype(f32).astype(bf16))
        off = u_ids - (cu + 4)
        weights = jnp.zeros((EU, BLK), f32)
        for a in range(TAPS):
            weights = jnp.where(off == a, ku[a:a + 1], weights)
        wu[...] = weights.astype(bf16)
        all_taps = jnp.concatenate([kv, jnp.broadcast_to(cv, (8, BLK)).astype(f32)], 0)
        taps[...] = all_taps
        wv[...] = v_weights(all_taps, 2 * span_s[0, c])

    def add_cells(v_at, wu, xt, wv):
        for j in range(0, GROUP, 2):
            rhs = jnp.concatenate([xt[...] * wv[i:i + 1] for i in (j, j + 1)], 0)
            add = lax.dot_general(wu[...], rhs, NT, preferred_element_type=f32)
            for i in range(2):
                at = pl.ds((v_at + j + i) * EU, EU)
                grid[at, :] = grid[at, :] + add[:, i * FEAT:(i + 1) * FEAT]

    prepare(0, sets[0])

    @pl.loop(0, (chunks + 1) // 2)
    def _(pair):
        for half in range(2):
            c = 2 * pair + half
            wu, taps, xt, wv = sets[half]
            v_first = 2 * span_s[0, c]
            steps = 2 * (span_s[1, c] - span_s[0, c]) + TAPS + 1
            prepare(jnp.minimum(c + 1, slots // BLK - 1), sets[1 - half])
            add_cells(v_first, wu, xt, wv[...])

            @pl.loop(1, (steps + GROUP - 1) // GROUP)
            def _(g):
                v_at = v_first + g * GROUP
                add_cells(v_at, wu, xt, v_weights(taps[...], v_at))

    ve_low[...] = grid[pl.ds(0, PAD * EU), :].astype(bf16)
    ve_high[...] = grid[pl.ds((TV + PAD) * EU, PAD * EU), :].astype(bf16)


def grid_rows(recv, table):
    sources = recv.shape[0]
    slots = sources * CAP
    vmem = pl.BlockSpec(memory_space=pltpu.VMEM)
    return pl.pallas_call(
        grid_kernel,
        in_specs=[vmem, pl.BlockSpec(memory_space=pltpu.HBM)],
        out_specs=(vmem, vmem, vmem),
        out_shape=(
            jax.ShapeDtypeStruct((EV, EU, FEAT), f32),
            jax.ShapeDtypeStruct((PAD * EU, FEAT), bf16),
            jax.ShapeDtypeStruct((PAD * EU, FEAT), bf16),
        ),
        scratch_shapes=[
            pltpu.VMEM((sources, CAP, FEAT), f32),
            pltpu.VMEM((slots, FEAT), f32),
            pltpu.VMEM((4 * slots // BLK, BLK), i32),
            pltpu.VMEM((sources, FEAT), f32),
            pltpu.VMEM((FEAT, sources), f32),
            pltpu.VMEM((slots // BLK, BLK // 2), i32),
            pltpu.SMEM((slots // BLK, BLK // 2), i32),
            pltpu.VMEM((8, 128), i32),
            pltpu.SMEM((8, 128), i32),
            pltpu.VMEM((EU, BLK), bf16),
            pltpu.VMEM((EU, BLK), bf16),
            pltpu.VMEM((16, BLK), f32),
            pltpu.VMEM((16, BLK), f32),
            pltpu.VMEM((FEAT, BLK), bf16),
            pltpu.VMEM((FEAT, BLK), bf16),
            pltpu.VMEM((GROUP + 4, BLK), bf16),
            pltpu.VMEM((GROUP + 4, BLK), bf16),
            pltpu.VMEM((TAPS, 128), bf16),
            pltpu.SemaphoreType.DMA((3,)),
        ],
        compiler_params=pltpu.CompilerParams(vmem_limit_bytes=24 * MIB),
        name="grid_rows",
    )(recv, table)


def edge_kernel(grid3, ue_ref, sem):
    def edge_copy(e, u):
        at = (PAD, TU + 8)[e] + u
        return pltpu.make_async_copy(grid3.at[pl.ds(PAD, TV), at], ue_ref.at[e, u], sem)

    edges = [edge_copy(e, u) for e in range(2) for u in range(PAD)]
    for copy in edges:
        copy.start()
    for copy in edges:
        copy.wait()


def u_edges(grid):
    vmem = pl.BlockSpec(memory_space=pltpu.VMEM)
    return pl.pallas_call(
        edge_kernel,
        in_specs=[vmem],
        out_specs=vmem,
        out_shape=jax.ShapeDtypeStruct((2, PAD, TV, FEAT), f32),
        scratch_shapes=[pltpu.SemaphoreType.DMA(())],
        compiler_params=pltpu.CompilerParams(vmem_limit_bytes=4 * MIB),
        cost_estimate=pl.CostEstimate(flops=10**8, bytes_accessed=2 * MIB, transcendentals=0),
        name="u_edges",
    )(grid)


def corner_kernel(low_ref, high_ref, ue_ref, send_low, send_high, low, high, edges):
    edges[...] = ue_ref[...]
    low[...] = low_ref[...].astype(f32)
    high[...] = high_ref[...].astype(f32)
    for e, (at, send) in enumerate(((PAD, send_low), (TU + 8, send_high))):
        for u in range(PAD):
            there = pl.ds(at + u, PAD, stride=EU)
            edges[e, u, 0:PAD, :] += low[there, :]
            edges[e, u, TV - PAD:TV, :] += high[there, :]
        send[...] = edges[e].astype(bf16)


def add_corners(low, high, ue):
    edge = jax.ShapeDtypeStruct(ue.shape[1:], bf16)
    return pl.pallas_call(
        corner_kernel,
        out_shape=(edge, edge),
        scratch_shapes=[
            pltpu.VMEM(low.shape, f32),
            pltpu.VMEM(high.shape, f32),
            pltpu.VMEM(ue.shape, f32),
        ],
        compiler_params=pltpu.CompilerParams(vmem_limit_bytes=8 * MIB),
        name="add_corners",
    )(low, high, ue)


def tile_kernel(grid_in, low_ref, high_ref, grid3, out_hbm, own_ref, sems):
    for at, halo in ((PAD, low_ref), (TV, high_ref)):
        for v in range(PAD):
            grid3[at + v] += halo[pl.ds(v * EU, EU), :].astype(f32)

    def out_copy(u):
        return pltpu.make_async_copy(grid3.at[pl.ds(PAD, TV), 8 + u], out_hbm.at[u], sems.at[0])

    def own_copy(e, u):
        at = 8 + e * (TU - PAD) + u
        return pltpu.make_async_copy(grid3.at[pl.ds(PAD, TV), at], own_ref.at[e, u], sems.at[1])

    ends = [own_copy(e, u) for e in range(2) for u in range(PAD)]
    for copy in ends:
        copy.start()

    @pl.loop(PAD, TU - PAD)
    def _(u):
        out_copy(u).start()

    for copy in ends:
        copy.wait()

    @pl.loop(PAD, TU - PAD)
    def _(u):
        out_copy(u).wait()


def write_tile(grid, low, high):
    vmem = pl.BlockSpec(memory_space=pltpu.VMEM)
    return pl.pallas_call(
        tile_kernel,
        in_specs=[vmem] * 3,
        out_specs=(vmem, pl.BlockSpec(memory_space=pltpu.HBM), vmem),
        out_shape=(
            jax.ShapeDtypeStruct(grid.shape, f32),
            jax.ShapeDtypeStruct((TU, TV, FEAT), f32),
            jax.ShapeDtypeStruct((2, PAD, TV, FEAT), f32),
        ),
        scratch_shapes=[pltpu.SemaphoreType.DMA((2,))],
        input_output_aliases={0: 0},
        compiler_params=pltpu.CompilerParams(vmem_limit_bytes=4 * MIB),
        name="write_tile",
    )(grid, low, high)


def u_edge_kernel(out_in, low_ref, high_ref, own_ref, out_hbm, edges, sems):
    def copy(e):
        return pltpu.make_async_copy(edges.at[e], out_hbm.at[pl.ds(e * (TU - PAD), PAD)], sems.at[e])

    edges[0] = own_ref[0] + low_ref[...].astype(f32)
    copy(0).start()
    edges[1] = own_ref[1] + high_ref[...].astype(f32)
    copy(1).start()
    copy(0).wait()
    copy(1).wait()


def add_u_edges(out, low, high, own):
    vmem = pl.BlockSpec(memory_space=pltpu.VMEM)
    hbm = pl.BlockSpec(memory_space=pl.ANY)
    return pl.pallas_call(
        u_edge_kernel,
        in_specs=[hbm, vmem, vmem, vmem],
        out_specs=hbm,
        out_shape=jax.ShapeDtypeStruct(out.shape, f32),
        scratch_shapes=[pltpu.VMEM(own.shape, f32), pltpu.SemaphoreType.DMA((2,))],
        input_output_aliases={0: 0},
        compiler_params=pltpu.CompilerParams(vmem_limit_bytes=8 * MIB),
        name="add_u_edges",
    )(out, low, high, own)


def shifted(x, axis, up):
    n = lax.axis_size(axis)
    pairs = [(i, i + 1) if up else (i + 1, i) for i in range(n - 1)]
    return lax.ppermute(x, axis, pairs)


def local(visibility, destination, cell_u, cell_v, tap_u, tap_v, kernel_table):
    axes = ("au", "vert")
    tiles = lax.axis_size("au") * lax.axis_size("vert")
    sent = pack(visibility, destination, cell_u, cell_v, tap_u, tap_v, tiles)
    recv = lax.all_to_all(sent, axes, split_axis=0, concat_axis=0, tiled=True)
    grid, ve_low, ve_high = grid_rows(recv, kernel_table.T)
    v_low = shifted(ve_high, "vert", True)
    v_high = shifted(ve_low, "vert", False)
    send_low, send_high = add_corners(v_low, v_high, u_edges(grid))
    u_low = shifted(send_high, "au", True)
    u_high = shifted(send_low, "au", False)
    _, out, own = write_tile(grid, v_low, v_high)
    return add_u_edges(out, u_low, u_high, own)


def solution(mesh):
    rows = P(("au", "vert"))
    return jax.shard_map(
        local,
        mesh=mesh,
        in_specs=(P(("au", "vert"), None), P(("au", "vert"), None), rows, rows, rows, rows, P()),
        out_specs=P("au", "vert", None),
        check_vma=False,
    )
```
